256 devices in a mesh: row: 32 (over y_hi, z, core), col: 8 (over y_lo, x).
Axes of the slice: x: 4, y: 4 (y_hi: 2, y_lo: 2; y = y_hi * 2 + y_lo), z: 8, core: 2. Of those that a mesh axis runs over, the one named last changes fastest.
Arguments:
- tokens: bfloat16 [256, 128, 256], P('row', 'col'), may hold values from -6 to 6
- gain_fine: float32 [256], replicated, may hold values from 0.1 to 1.9
- qkv_fine: bfloat16 [256, 768], replicated, may hold values from -0.375 to 0.375
- out_fine: bfloat16 [256, 256], replicated, may hold values from -0.375 to 0.375
- w_merge: bfloat16 [1024, 512], replicated, may hold values from -0.1875 to 0.1875
- gain_coarse: float32 [512], replicated, may hold values from 0.1 to 1.9
- qkv_coarse: bfloat16 [512, 1536], replicated, may hold values from -0.25 to 0.25
- out_coarse: bfloat16 [512, 512], replicated, may hold values from -0.25 to 0.25
- grad_fine: bfloat16 [256, 128, 256], P('row', 'col'), may hold values from -6 to 6
- grad_coarse: bfloat16 [128, 64, 512], P('row', 'col'), may hold values from -6 to 6
Outputs:
- grad_tokens: bfloat16 [256, 128, 256], P('row', 'col')
- grad_gain_fine: float32 [256], replicated
- grad_qkv_fine: bfloat16 [256, 768], replicated
- grad_out_fine: bfloat16 [256, 256], replicated
- grad_merge: bfloat16 [1024, 512], replicated
- grad_gain_coarse: float32 [512], replicated
- grad_qkv_coarse: bfloat16 [512, 1536], replicated
- grad_out_coarse: bfloat16 [512, 512], replicated
The draws below stay inside these ranges and needn't reach their ends.
All inputs are finite; a program needn't handle non-finite values.
Results may differ from the reference program's by a relative error of at most 0.035.
Values may be sent and summed in bfloat16 or wider, within the bound.
No kernel may reach another device: no remote copies, remote signals or barrier semaphores. Data moves between devices by JAX's collectives and lax.ppermute only.
A program may use at most 64 MiB of HBM per device.

```python
import math
import jax
import jax.numpy as jnp
from jax import lax

D0 = 256
D1 = 512
HEAD = 64
RADIUS = 3
ROWS0 = 256
COLS0 = 128
ROWS1 = 128
COLS1 = 64


def levels(stream_key, dims, cuts, low, top_value):
    loudness = 1.0
    for dim, blocks in cuts:
        heights = jax.random.uniform(jax.random.fold_in(jax.random.fold_in(stream_key, 6), dim), (blocks,), jnp.float32, low / len(cuts), top_value / len(cuts))
        loudness = loudness * jnp.repeat(jnp.exp(heights), dims[dim] // blocks).reshape((-1,) + (1,) * (len(dims) - 1 - dim))
    return loudness


def gaussian(rng, shape, spread, bound, pieces=(), held_as=jnp.bfloat16):
    array = spread * jax.random.normal(rng, shape, jnp.float32)
    if pieces:
        array = array * levels(rng, shape, pieces, -0.22, 0.18)
    return jnp.clip(array, -bound, bound).astype(held_as)


def setup_inputs(seed: int = 0) -> dict:
    splits = jax.random.split(jax.random.key(seed), 11)
    tokens = gaussian(splits[0], (ROWS0, COLS0, D0), 1.0, 6.0, ((0, 32), (1, 8)))
    gain_fine = jnp.clip(1.0 + 0.18 * jax.random.normal(splits[1], (D0,), jnp.float32), 0.1, 1.9)
    qkv_fine = gaussian(splits[2], (D0, 3 * D0), D0 ** -0.5, 0.375)
    out_fine = gaussian(splits[3], (D0, D0), D0 ** -0.5, 0.375)
    w_merge = gaussian(splits[4], (4 * D0, D1), (4 * D0) ** -0.5, 0.1875)
    gain_coarse = jnp.clip(1.0 + 0.18 * jax.random.normal(splits[5], (D1,), jnp.float32), 0.1, 1.9)
    qkv_coarse = gaussian(splits[6], (D1, 3 * D1), D1 ** -0.5, 0.25)
    out_coarse = gaussian(splits[7], (D1, D1), D1 ** -0.5, 0.25)
    grad_fine = gaussian(splits[8], (ROWS0, COLS0, D0), 1.0, 6.0, ((0, 32), (1, 8)))
    grad_coarse = gaussian(splits[9], (ROWS1, COLS1, D1), 1.0, 6.0, ((0, 32), (1, 8)))
    return dict(tokens=tokens, gain_fine=gain_fine, qkv_fine=qkv_fine, out_fine=out_fine, w_merge=w_merge, gain_coarse=gain_coarse, qkv_coarse=qkv_coarse, out_coarse=out_coarse, grad_fine=grad_fine, grad_coarse=grad_coarse)


norm_eps = 1e-06

def norm_forward(tokens, gain):
    values = tokens.astype(jnp.float32)
    scale = lax.rsqrt(lax.optimization_barrier(jnp.mean(values * values, axis=-1, keepdims=True)) + norm_eps)
    normed = (values * scale * gain).astype(jnp.bfloat16)
    return (values, scale, normed)

def norm_backward(values, scale, gain, upstream):
    gain_part = lax.optimization_barrier(jnp.sum(upstream * values * scale, axis=(0, 1)))
    weighted = upstream * gain
    inner = lax.optimization_barrier(jnp.mean(weighted * values, axis=-1, keepdims=True))
    return (weighted * scale - values * (scale * scale * scale) * inner, gain_part)

def pad_rim(field):
    return jnp.pad(field, ((RADIUS, RADIUS), (RADIUS, RADIUS), (0, 0)))

def offsets():
    extent = 2 * RADIUS + 1
    return [(down, across) for down in range(extent) for across in range(extent)]

def attention_forward(query, keys, values_in, heads):
    rows, columns, width = query.shape
    head_dim = width // heads
    factor = 1.0 / math.sqrt(head_dim)
    query_heads = query.astype(jnp.float32).reshape(rows, columns, heads, head_dim)
    keys_pad = pad_rim(keys)
    values_pad = pad_rim(values_in)
    inside = pad_rim(jnp.ones((rows, columns, 1), jnp.float32))
    score_list = []
    valid_list = []
    for down, across in offsets():
        key_slice = keys_pad[down:down + rows, across:across + columns].astype(jnp.float32).reshape(rows, columns, heads, head_dim)
        score_list.append(lax.optimization_barrier(jnp.sum(query_heads * key_slice, axis=-1)) * factor)
        valid_list.append(inside[down:down + rows, across:across + columns])
    scores = jnp.stack(score_list, axis=-1)
    valid = jnp.stack(valid_list, axis=-1)
    weights = jnp.where(valid > 0.5, jnp.exp(scores), 0.0)
    probability = weights / lax.optimization_barrier(jnp.sum(weights, axis=-1, keepdims=True))
    probability_b = probability.astype(jnp.bfloat16)
    probability_f = lax.optimization_barrier(probability_b).astype(jnp.float32)
    attended = jnp.zeros((rows, columns, heads, head_dim), jnp.float32)
    for place, (down, across) in enumerate(offsets()):
        value_slice = values_pad[down:down + rows, across:across + columns].astype(jnp.float32).reshape(rows, columns, heads, head_dim)
        attended = attended + probability_f[..., place:place + 1] * value_slice
    attended = attended.astype(jnp.bfloat16).reshape(rows, columns, width)
    return (attended, probability, probability_f)

def attention_backward(query, keys, values_in, heads, probability, probability_f, grad_att):
    rows, columns, width = query.shape
    head_dim = width // heads
    factor = 1.0 / math.sqrt(head_dim)
    query_heads = query.astype(jnp.float32).reshape(rows, columns, heads, head_dim)
    grad_heads = grad_att.astype(jnp.float32).reshape(rows, columns, heads, head_dim)
    keys_pad = pad_rim(keys)
    values_pad = pad_rim(values_in)
    dprob_list = []
    for down, across in offsets():
        value_slice = values_pad[down:down + rows, across:across + columns].astype(jnp.float32).reshape(rows, columns, heads, head_dim)
        dprob_list.append(lax.optimization_barrier(jnp.sum(grad_heads * value_slice, axis=-1)))
    dprob = jnp.stack(dprob_list, axis=-1)
    total = lax.optimization_barrier(jnp.sum(probability * dprob, axis=-1, keepdims=True))
    dscore_b = (probability * (dprob - total) * factor).astype(jnp.bfloat16)
    dscore = lax.optimization_barrier(dscore_b).astype(jnp.float32)
    grad_query = jnp.zeros((rows, columns, heads, head_dim), jnp.float32)
    grad_keys = jnp.zeros((rows + 2 * RADIUS, columns + 2 * RADIUS, heads, head_dim), jnp.float32)
    grad_values = jnp.zeros((rows + 2 * RADIUS, columns + 2 * RADIUS, heads, head_dim), jnp.float32)
    for place, (down, across) in enumerate(offsets()):
        key_slice = keys_pad[down:down + rows, across:across + columns].astype(jnp.float32).reshape(rows, columns, heads, head_dim)
        grad_query = grad_query + dscore[..., place:place + 1] * key_slice
        grad_keys = grad_keys.at[down:down + rows, across:across + columns].add(dscore[..., place:place + 1] * query_heads)
        grad_values = grad_values.at[down:down + rows, across:across + columns].add(probability_f[..., place:place + 1] * grad_heads)
    grad_keys = grad_keys[RADIUS:RADIUS + rows, RADIUS:RADIUS + columns].reshape(rows, columns, width)
    grad_values = grad_values[RADIUS:RADIUS + rows, RADIUS:RADIUS + columns].reshape(rows, columns, width)
    return (grad_query.reshape(rows, columns, width), grad_keys, grad_values)

def level_forward(tokens, gain, w_qkv):
    width = tokens.shape[-1]
    heads = width // HEAD
    values, scale, normed = norm_forward(tokens, gain)
    projected = jnp.dot(normed, w_qkv, preferred_element_type=jnp.float32).astype(jnp.bfloat16)
    query = projected[..., :width]
    keys = projected[..., width:2 * width]
    values_in = projected[..., 2 * width:]
    attended, probability, probability_f = attention_forward(query, keys, values_in, heads)
    return (attended, (values, scale, normed, attended, query, keys, values_in, probability, probability_f, heads))

def level_backward(stored, upstream, gain, w_qkv, w_out):
    values, scale, normed, attended, query, keys, values_in, probability, probability_f, heads = stored
    width = values.shape[-1]
    upstream_b = upstream.astype(jnp.bfloat16)
    grad_out = jnp.dot(attended.reshape(-1, width).T, upstream_b.reshape(-1, width), preferred_element_type=jnp.float32)
    grad_att = jnp.dot(upstream_b, w_out.T, preferred_element_type=jnp.float32).astype(jnp.bfloat16)
    grad_query, grad_keys, grad_values = attention_backward(query, keys, values_in, heads, probability, probability_f, grad_att)
    grad_proj = jnp.concatenate([grad_query, grad_keys, grad_values], axis=-1).astype(jnp.bfloat16)
    grad_qkv = jnp.dot(normed.reshape(-1, width).T, grad_proj.reshape(-1, 3 * width), preferred_element_type=jnp.float32)
    grad_normed = jnp.dot(grad_proj, w_qkv.T, preferred_element_type=jnp.float32)
    grad_inputs, grad_gain = norm_backward(values, scale, gain, grad_normed)
    return (upstream + grad_inputs, grad_qkv, grad_out, grad_gain)

def merge_tokens(field):
    rows, columns, width = field.shape
    shaped = field.reshape(rows // 2, 2, columns // 2, 2, width).transpose(0, 2, 1, 3, 4)
    return shaped.reshape(rows // 2, columns // 2, 4 * width)

def split_tokens(field):
    rows, columns, width = field.shape
    shaped = field.reshape(rows, columns, 2, 2, width // 4).transpose(0, 2, 1, 3, 4)
    return shaped.reshape(2 * rows, 2 * columns, width // 4)

def reference(tokens, gain_fine, qkv_fine, out_fine, w_merge, gain_coarse, qkv_coarse, out_coarse, grad_fine, grad_coarse):
    attended_fine, stored_fine = level_forward(tokens, gain_fine, qkv_fine)
    fine_out = (stored_fine[0] + jnp.dot(attended_fine, out_fine, preferred_element_type=jnp.float32)).astype(jnp.bfloat16)
    merged = merge_tokens(fine_out)
    coarse_in = jnp.dot(merged, w_merge, preferred_element_type=jnp.float32).astype(jnp.bfloat16)
    attended_coarse, stored_coarse = level_forward(coarse_in, gain_coarse, qkv_coarse)
    grad_coarse_in, grad_qkv1, grad_out1, grad_gain1 = level_backward(stored_coarse, grad_coarse.astype(jnp.float32), gain_coarse, qkv_coarse, out_coarse)
    coarse_b = grad_coarse_in.astype(jnp.bfloat16)
    merge_width = merged.shape[-1]
    grad_merge = jnp.dot(merged.reshape(-1, merge_width).T, coarse_b.reshape(-1, coarse_b.shape[-1]), preferred_element_type=jnp.float32)
    grad_merged = jnp.dot(coarse_b, w_merge.T, preferred_element_type=jnp.float32)
    grad_fine_total = grad_fine.astype(jnp.float32) + split_tokens(grad_merged)
    grad_tokens, grad_qkv0, grad_out0, grad_gain0 = level_backward(stored_fine, grad_fine_total, gain_fine, qkv_fine, out_fine)
    factor = 1.0 / math.sqrt(ROWS0 * COLS0)
    return (grad_tokens.astype(jnp.bfloat16), grad_gain0 * factor, (grad_qkv0 * factor).astype(jnp.bfloat16), (grad_out0 * factor).astype(jnp.bfloat16), (grad_merge * factor).astype(jnp.bfloat16), grad_gain1 * factor, (grad_qkv1 * factor).astype(jnp.bfloat16), (grad_out1 * factor).astype(jnp.bfloat16))
```

```python
import math

import jax
import jax.numpy as jnp
from jax import lax
from jax.sharding import PartitionSpec as P

HEAD = 64
RADIUS = 3


norm_eps = 1e-06


def shifted(x, axis, by):
    count = lax.axis_size(axis)
    pairs = [(i, i + by) for i in range(count) if 0 <= i + by < count]
    return lax.ppermute(x, axis, pairs)


def extended_2(x, sides, width):
    for axis, dim in sides:
        count, length = (lax.axis_size(axis), x.shape[dim])
        up = [(i, (i + 1) % count) for i in range(count - 1)]
        down = [(j, i) for i, j in up]
        last = lax.slice_in_dim(x, length - width, length, axis=dim)
        leading = lax.slice_in_dim(x, 0, width, axis=dim)
        before = lax.ppermute(last, axis, up)
        after = lax.ppermute(leading, axis, down)
        x = jnp.concatenate([before, x, after], axis=dim)
    return x


def norm_forward(tokens, gain):
    values = tokens.astype(jnp.float32)
    scale = lax.rsqrt(jnp.mean(values * values, axis=-1, keepdims=True) + norm_eps)
    normed = (values * scale * gain).astype(jnp.bfloat16)
    return (values, scale, normed)


def norm_backward(values, scale, gain, upstream):
    gain_part = jnp.sum(upstream * values * scale, axis=(0, 1))
    weighted = upstream * gain
    inner = jnp.mean(weighted * values, axis=-1, keepdims=True)
    return (weighted * scale - values * (scale * scale * scale) * inner, gain_part)


def key_validity(rows, columns):
    row_ids = lax.axis_index("row") * rows - RADIUS + jnp.arange(rows + 2 * RADIUS)
    col_ids = lax.axis_index("col") * columns - RADIUS + jnp.arange(columns + 2 * RADIUS)
    row_ok = (row_ids >= 0) & (row_ids < rows * lax.axis_size("row"))
    col_ok = (col_ids >= 0) & (col_ids < columns * lax.axis_size("col"))
    return row_ok[:, None] & col_ok[None, :]


def block_layout(columns):
    block = math.gcd(columns, 16)
    return (block, columns // block, block + 2 * RADIUS)


def split_blocks(extended):
    return jnp.stack([extended], axis=1)


def stack_window(extended, rows):
    return jnp.stack([extended[down : down + rows] for down in range(2 * RADIUS + 1)], axis=2)


def attention_forward(query, kv_ext, valid_ext, heads):
    rows, columns, width = query.shape
    head_dim = width // heads
    extent = 2 * RADIUS + 1
    block, count, wide = block_layout(columns)
    keys_all = extent * wide
    factor = 1.0 / math.sqrt(head_dim)
    window = stack_window(split_blocks(kv_ext), rows).reshape(
        rows, count, keys_all, 2, heads, head_dim
    )
    keys = window[:, :, :, 0]
    values_win = window[:, :, :, 1]
    seen = stack_window(split_blocks(valid_ext), rows).reshape(rows, count, 1, 1, keys_all)
    key_col = jnp.tile(jnp.arange(wide), extent)
    offset = key_col[None, :] - jnp.arange(block)[:, None]
    band = (offset >= 0) & (offset <= 2 * RADIUS)
    mask = band[None, None, None] & seen
    query_heads = query.reshape(rows, count, block, heads, head_dim)
    scores = (
        jnp.einsum("rnchd,rnkhd->rnhck", query_heads, keys, preferred_element_type=jnp.float32)
        * factor
    )
    weights = jnp.where(mask, jnp.exp(scores), 0.0)
    probability = weights / jnp.sum(weights, axis=-1, keepdims=True)
    probability_b = probability.astype(jnp.bfloat16)
    attended = jnp.einsum(
        "rnhck,rnkhd->rnchd", probability_b, values_win, preferred_element_type=jnp.float32
    )
    attended = attended.astype(jnp.bfloat16).reshape(rows, columns, width)
    return (attended, (query_heads, keys, values_win, probability, probability_b, factor))


def attention_backward(saved, grad_att):
    query_heads, keys, values_win, probability, probability_b, factor = saved
    rows, count, block, heads, head_dim = query_heads.shape
    width = heads * head_dim
    columns = count * block
    extent = 2 * RADIUS + 1
    wide = block + 2 * RADIUS
    span = columns + 2 * RADIUS
    grad_heads = grad_att.reshape(rows, count, block, heads, head_dim)
    dprob = jnp.einsum(
        "rnchd,rnkhd->rnhck", grad_heads, values_win, preferred_element_type=jnp.float32
    )
    total = jnp.sum(probability * dprob, axis=-1, keepdims=True)
    dscore = (probability * (dprob - total) * factor).astype(jnp.bfloat16)
    grad_query = jnp.einsum(
        "rnhck,rnkhd->rnchd", dscore, keys, preferred_element_type=jnp.float32
    ).reshape(rows, columns, width)
    grad_keys = jnp.einsum(
        "rnhck,rnchd->rnkhd", dscore, query_heads, preferred_element_type=jnp.float32
    )
    grad_values = jnp.einsum(
        "rnhck,rnchd->rnkhd", probability_b, grad_heads, preferred_element_type=jnp.float32
    )
    grad_window = jnp.concatenate(
        [
            grad_keys.reshape(rows, count, extent, wide, width),
            grad_values.reshape(rows, count, extent, wide, width),
        ],
        axis=-1,
    )
    grad_blocks = jnp.zeros((rows + 2 * RADIUS, count, wide, 2 * width), jnp.float32)
    for down in range(extent):
        grad_blocks = grad_blocks.at[down : down + rows].add(grad_window[:, :, down])
    grad_ext = jnp.zeros((rows + 2 * RADIUS, span, 2 * width), jnp.float32)
    grad_ext = grad_ext.at[:, 0:wide].add(grad_blocks[:, 0])
    return (grad_query, grad_ext)


def fold_rims(grad_ext):
    rows = grad_ext.shape[0] - 2 * RADIUS
    columns = grad_ext.shape[1] - 2 * RADIUS
    left_rim = grad_ext[:, :RADIUS]
    right_rim = grad_ext[:, columns + RADIUS :]
    middle = grad_ext[:, RADIUS : columns + RADIUS]
    from_next = shifted(left_rim.astype(jnp.bfloat16), "col", -1).astype(left_rim.dtype)
    from_prev = shifted(right_rim.astype(jnp.bfloat16), "col", 1).astype(right_rim.dtype)
    middle = middle.at[:, columns - RADIUS :].add(from_next).at[:, :RADIUS].add(from_prev)
    top_rim = middle[:RADIUS]
    bottom_rim = middle[rows + RADIUS :]
    center = middle[RADIUS : rows + RADIUS]
    from_below = shifted(top_rim.astype(jnp.bfloat16), "row", -1).astype(top_rim.dtype)
    from_above = shifted(bottom_rim.astype(jnp.bfloat16), "row", 1).astype(bottom_rim.dtype)
    return center.at[rows - RADIUS :].add(from_below).at[:RADIUS].add(from_above)


def level_forward(tokens, gain, w_qkv):
    rows, columns, width = tokens.shape
    heads = width // HEAD
    values, scale, normed = norm_forward(tokens, gain)
    projected = jnp.dot(normed, w_qkv, preferred_element_type=jnp.float32).astype(jnp.bfloat16)
    query = projected[..., :width]
    kv_ext = extended_2(projected[..., width:], (("row", 0), ("col", 1)), RADIUS)
    attended, saved = attention_forward(query, kv_ext, key_validity(rows, columns), heads)
    return (attended, (values, scale, normed, attended, saved))


def level_backward(stored, upstream, gain, w_qkv, w_out):
    values, scale, normed, attended, saved = stored
    upstream_b = upstream.astype(jnp.bfloat16)
    grad_out = jnp.einsum("rcd,rce->de", attended, upstream_b, preferred_element_type=jnp.float32)
    grad_att = jnp.einsum(
        "rce,de->rcd", upstream_b, w_out, preferred_element_type=jnp.float32
    ).astype(jnp.bfloat16)
    grad_query, grad_ext = attention_backward(saved, grad_att)
    grad_kv = fold_rims(grad_ext)
    grad_proj = jnp.concatenate([grad_query, grad_kv], axis=-1).astype(jnp.bfloat16)
    grad_qkv = jnp.einsum("rcd,rce->de", normed, grad_proj, preferred_element_type=jnp.float32)
    grad_normed = jnp.einsum("rce,de->rcd", grad_proj, w_qkv, preferred_element_type=jnp.float32)
    grad_inputs, grad_gain = norm_backward(values, scale, gain, grad_normed)
    return (upstream + grad_inputs, grad_qkv, grad_out, grad_gain)


def merge_tokens(field):
    rows, columns, width = field.shape
    shaped = field.reshape(rows // 2, 2, columns // 2, 2, width).transpose(0, 2, 1, 3, 4)
    return shaped.reshape(rows // 2, columns // 2, 4 * width)


def split_tokens(field):
    rows, columns, width = field.shape
    shaped = field.reshape(rows, columns, 2, 2, width // 4).transpose(0, 2, 1, 3, 4)
    return shaped.reshape(2 * rows, 2 * columns, width // 4)


def flip(x, axis, bit):
    return lax.ppermute(x, axis, [(i, i ^ bit) for i in range(lax.axis_size(axis))])


def to_rows(field):
    rows, columns = field.shape
    if columns == 256:
        return field.reshape(2, rows // 2, 256).transpose(1, 0, 2).reshape(rows // 2, 512)
    if columns == 768:
        return jnp.concatenate([field[:, :512], to_rows(field[:, 512:])], axis=0)
    return jnp.concatenate([field[:, c : c + 512] for c in range(0, columns, 512)], axis=0)


def from_rows(flat, rows, columns):
    if columns == 256:
        return flat.reshape(rows // 2, 2, 256).transpose(1, 0, 2).reshape(rows, 256)
    if columns == 768:
        return jnp.concatenate([flat[:rows], from_rows(flat[rows:], rows, 256)], axis=1)
    parts = [flat[r : r + rows] for r in range(0, flat.shape[0], rows)]
    return jnp.concatenate(parts, axis=1)


def own_half(x, axis, bit):
    half = x.shape[0] // 2
    mine = (lax.axis_index(axis) // bit) % 2
    keep = lax.dynamic_slice_in_dim(x, mine * half, half, axis=0)
    send = lax.dynamic_slice_in_dim(x, (1 - mine) * half, half, axis=0)
    return keep, send


def add_b(a, b):
    return (a.astype(jnp.float32) + b.astype(jnp.float32)).astype(jnp.bfloat16)


def halve(x, small, axis, bit):
    keep, send = own_half(x, axis, bit)
    got = flip(jnp.concatenate([send, small], axis=0), axis, bit)
    half = keep.shape[0]
    return add_b(keep, got[:half]), add_b(small, got[half:])


def rejoin(x, axis, bit):
    mine = (lax.axis_index(axis) // bit) % 2
    other = flip(x, axis, bit)
    return jnp.where(mine == 0, jnp.concatenate([x, other]), jnp.concatenate([other, x]))


def reduce_weights(grads, gains):
    packed = jnp.concatenate([to_rows(g.astype(jnp.bfloat16)) for g in grads], axis=0)
    lengths = [g.shape[0] for g in gains]
    small = jnp.pad(jnp.concatenate(gains), (0, 16 * 512 - sum(lengths)))
    small = small.reshape(16, 512).astype(jnp.bfloat16)
    x, small = halve(packed, small, "row", 1)
    count = lax.axis_size("col")
    pieces = x.reshape(count, -1, 512)
    pieces = jnp.concatenate([pieces, jnp.broadcast_to(small, (count, 16, 512))], axis=1)
    pieces = lax.all_to_all(pieces, "col", 0, 0)
    total = jnp.sum(pieces.astype(jnp.float32), axis=0).astype(jnp.bfloat16)
    x, small = total[:-16], total[-16:]
    x, small = halve(x, small, "row", 2)
    x = jnp.concatenate([x, small], axis=0)
    for bit in (4, 8, 16):
        x = add_b(x, flip(x, "row", bit))
    x, small = x[:-16], x[-16:]
    x = rejoin(x, "row", 2)
    x = lax.all_to_all(jnp.broadcast_to(x, (count,) + x.shape), "col", 0, 0)
    x = rejoin(x.reshape(-1, 512), "row", 1)
    out, place = [], 0
    for g in grads:
        rows = g.shape[0] * g.shape[1] // 512
        out.append(from_rows(x[place : place + rows], *g.shape))
        place += rows
    small = small.astype(jnp.float32).reshape(-1)
    ends = [0]
    for n in lengths:
        ends.append(ends[-1] + n)
    return out, [small[a:b] for a, b in zip(ends, ends[1:])]


def per_device(
    tokens,
    gain_fine,
    qkv_fine,
    out_fine,
    w_merge,
    gain_coarse,
    qkv_coarse,
    out_coarse,
    grad_fine,
    grad_coarse,
):
    rows, columns, width_fine = tokens.shape
    attended_fine, stored_fine = level_forward(tokens, gain_fine, qkv_fine)
    fine_out = (
        stored_fine[0] + jnp.dot(attended_fine, out_fine, preferred_element_type=jnp.float32)
    ).astype(jnp.bfloat16)
    merged = merge_tokens(fine_out)
    coarse_in = jnp.dot(merged, w_merge, preferred_element_type=jnp.float32).astype(jnp.bfloat16)
    attended_coarse, stored_coarse = level_forward(coarse_in, gain_coarse, qkv_coarse)
    grad_coarse_in, grad_qkv1, grad_out1, grad_gain1 = level_backward(
        stored_coarse, grad_coarse.astype(jnp.float32), gain_coarse, qkv_coarse, out_coarse
    )
    coarse_b = grad_coarse_in.astype(jnp.bfloat16)
    grad_merge = jnp.einsum("rcm,rce->me", merged, coarse_b, preferred_element_type=jnp.float32)
    grad_merged = jnp.einsum("rce,me->rcm", coarse_b, w_merge, preferred_element_type=jnp.float32)
    grad_fine_total = grad_fine.astype(jnp.float32) + split_tokens(grad_merged)
    grad_tokens, grad_qkv0, grad_out0, grad_gain0 = level_backward(
        stored_fine, grad_fine_total, gain_fine, qkv_fine, out_fine
    )
    grads = (grad_qkv0, grad_out0, grad_merge, grad_qkv1, grad_out1)
    summed, gains = reduce_weights(grads, (grad_gain0, grad_gain1))
    grad_qkv0, grad_out0, grad_merge, grad_qkv1, grad_out1 = summed
    grad_gain0, grad_gain1 = gains
    factor = 1.0 / math.sqrt(rows * lax.axis_size("row") * columns * lax.axis_size("col"))
    return (
        grad_tokens.astype(jnp.bfloat16),
        grad_gain0 * factor,
        (grad_qkv0 * factor).astype(jnp.bfloat16),
        (grad_out0 * factor).astype(jnp.bfloat16),
        (grad_merge * factor).astype(jnp.bfloat16),
        grad_gain1 * factor,
        (grad_qkv1 * factor).astype(jnp.bfloat16),
        (grad_out1 * factor).astype(jnp.bfloat16),
    )


def solution(mesh):
    in_specs = (
        P("row", "col", None),
        P(),
        P(),
        P(),
        P(),
        P(),
        P(),
        P(),
        P("row", "col", None),
        P("row", "col", None),
    )
    out_specs = (P("row", "col", None), P(), P(), P(), P(), P(), P(), P())
    return jax.shard_map(
        per_device, mesh=mesh, in_specs=in_specs, out_specs=out_specs, check_vma=False
    )
```

```python
import functools
import math

import jax
import jax.numpy as jnp
import numpy as np
from jax import lax
from jax.experimental import pallas as pl
from jax.experimental.pallas import tpu as pltpu
from jax.sharding import PartitionSpec as P

HEAD = 64
RADIUS = 3
PAIR = 2 * HEAD
NEG = -1e30
norm_eps = 1e-06
f32 = jnp.float32
bf16 = jnp.bfloat16


def shifted(x, axis, by):
    count = lax.axis_size(axis)
    pairs = [(i, i + by) for i in range(count) if 0 <= i + by < count]
    return lax.ppermute(x, axis, pairs)


def flip(x, axis, bit):
    return lax.ppermute(x, axis, [(i, i ^ bit) for i in range(lax.axis_size(axis))])


def add_b(a, b):
    return (a.astype(f32) + b.astype(f32)).astype(bf16)


def grid_piece(rows, columns, length=None):
    piece = [(r, c) for r in rows for c in columns]
    return piece + [None] * ((length or len(piece)) - len(piece))


def merge_order(rows, columns):
    return [
        (2 * a + rp, 2 * b + cp)
        for rp in (0, 1)
        for cp in (0, 1)
        for a in range(rows // 2)
        for b in range(columns // 2)
    ]


def fine_keys(rows, columns):
    reach = RADIUS
    tall = range(-reach, rows + reach)
    side = -(-len(tall) * reach // 16) * 16
    return [
        merge_order(rows, columns),
        grid_piece(range(-reach, 0), range(columns)),
        grid_piece(range(rows, rows + reach), range(columns)),
        grid_piece(tall, range(-reach, 0), side),
        grid_piece(tall, range(columns, columns + reach), side),
    ]


def coarse_keys(rows, columns):
    reach = 2 * RADIUS
    tall = range(-reach, rows + reach)
    return [
        grid_piece(range(rows), range(columns)),
        grid_piece(range(-rows, 0), range(columns)),
        grid_piece(range(rows, 2 * rows), range(columns)),
        grid_piece(range(-reach, -rows), range(columns)),
        grid_piece(range(2 * rows, rows + reach), range(columns)),
        grid_piece(tall, range(-reach, 0)),
        grid_piece(tall, range(columns, columns + reach)),
    ]


def coarse_queries(rows, columns):
    reach = RADIUS
    tall = range(-reach, rows + reach)
    side = -(-len(tall) * reach // 8) * 8
    return [
        grid_piece(range(rows), range(columns)),
        grid_piece(range(-reach, 0), range(columns)),
        grid_piece(range(rows, rows + reach), range(columns)),
        grid_piece(tall, range(-reach, 0), side),
        grid_piece(tall, range(columns, columns + reach), side),
    ]


def joined(pieces):
    return [place for piece in pieces for place in piece]


def band_bias(queries, keys):
    bias = np.full((len(queries), len(keys)), NEG, np.float32)
    for i, q in enumerate(queries):
        for j, k in enumerate(keys):
            if q is None:
                inside = j == 0
            else:
                inside = k is not None and max(abs(q[0] - k[0]), abs(q[1] - k[1])) <= RADIUS
            if inside:
                bias[i, j] = 0.0
    return bias


def key_bias(keys, rows, columns):
    row = np.array([k[0] if k else 0 for k in keys], np.int32)
    col = np.array([k[1] if k else 0 for k in keys], np.int32)
    row_ids = lax.axis_index("row") * rows + row
    col_ids = lax.axis_index("col") * columns + col
    ok = (row_ids >= 0) & (row_ids < rows * lax.axis_size("row"))
    ok &= (col_ids >= 0) & (col_ids < columns * lax.axis_size("col"))
    return jnp.where(ok, 0.0, NEG).astype(f32)[None, :]


def one_hot(targets, sources):
    place = {s: j for j, s in enumerate(sources) if s is not None}
    matrix = np.zeros((len(targets), len(sources)), np.float32)
    for i, t in enumerate(targets):
        if t is not None and t in place:
            matrix[i, place[t]] = 1.0
    return matrix.astype(jnp.bfloat16)


def dot(a, b):
    return jnp.dot(a, b, preferred_element_type=f32)


def dot_nt(a, b):
    return lax.dot_general(a, b, (((1,), (1,)), ((), ())), preferred_element_type=f32)


def dot_tn(a, b):
    return lax.dot_general(a, b, (((0,), (0,)), ((), ())), preferred_element_type=f32)


def norm_forward(x, gain):
    values = x.astype(f32)
    scale = lax.rsqrt(jnp.mean(values * values, axis=-1, keepdims=True) + norm_eps)
    return values, scale, (values * scale * gain).astype(bf16)


def norm_backward(values, scale, gain, upstream):
    gain_part = jnp.sum(upstream * values * scale, axis=0, keepdims=True)
    weighted = upstream * gain
    inner = jnp.mean(weighted * values, axis=-1, keepdims=True)
    return weighted * scale - values * (scale * scale * scale) * inner, gain_part


def head_masks():
    lane = lax.broadcasted_iota(jnp.int32, (1, PAIR), 1)
    return [(lane < HEAD).astype(f32), (lane >= HEAD).astype(f32)]


def masked(x, mask):
    return (x.astype(f32) * mask).astype(bf16)


def probabilities(query, keys, bias):
    weights = jnp.exp(dot_nt(query, keys) * (1.0 / math.sqrt(HEAD)) + bias)
    return weights / jnp.sum(weights, axis=-1, keepdims=True)


def score_gradient(prob, dprob):
    total = jnp.sum(prob * dprob, axis=-1, keepdims=True)
    return (prob * (dprob - total) * (1.0 / math.sqrt(HEAD))).astype(bf16)


def lanes(x, place):
    return x[:, place * PAIR : (place + 1) * PAIR]


def fine_forward_kernel(
    tok, top, bottom, left, right, perm, gain, w_qkv, w_out, w_merge, band, valid,
    merged_out, coarse_out, normed_out, proj_out, kv_out, att_out,
):
    width = tok.shape[1]
    own = dot(perm[...], tok[...]).astype(bf16)
    field = jnp.concatenate([own, top[...], bottom[...], left[...], right[...]], axis=0)
    _, _, normed = norm_forward(field, gain[...])
    count = own.shape[0]
    normed_out[...] = normed[:count]
    query = dot(normed[:count], w_qkv[:, :width]).astype(bf16)
    kv = dot(normed, w_qkv[:, width:]).astype(bf16)
    proj_out[...] = query
    kv_out[...] = kv
    bias = band[...] + valid[...]
    masks = head_masks()
    parts = []
    for p in range(width // PAIR):
        keys, vals, q = lanes(kv, p), lanes(kv, width // PAIR + p), lanes(query, p)
        total = None
        for mask in masks:
            prob = probabilities(masked(q, mask), keys, bias)
            part = dot(prob.astype(bf16), vals) * mask
            total = part if total is None else total + part
        parts.append(total.astype(bf16))
    attended = jnp.concatenate(parts, axis=1)
    att_out[...] = attended
    fine = (own.astype(f32) + dot(attended, w_out[...])).astype(bf16)
    quarter = count // 4
    acc = None
    for p in range(4):
        block = fine[p * quarter : (p + 1) * quarter]
        merged_out[:, p * width : (p + 1) * width] = block
        part = dot(block, w_merge[p * width : (p + 1) * width, :])
        acc = part if acc is None else acc + part
    coarse_out[...] = acc.astype(bf16)


def coarse_kernel(
    field, upstream, merged, pick, gain, w_qkv, w_out, w_merge, band, valid, parity,
    keep_out, send_out, gain_out, grad_merged_out,
):
    own, width = merged.shape[0], field.shape[1]
    pairs = width // PAIR
    values, scale, normed = norm_forward(field[...], gain[...])
    kv = dot(normed, w_qkv[:, width:]).astype(bf16)
    picked = dot(pick[...], normed).astype(bf16)
    query = dot(picked, w_qkv[:, :width]).astype(bf16)
    u_b = upstream[...]
    grad_att = dot_nt(u_b, w_out[...]).astype(bf16)
    bias = band[...] + valid[...]
    masks = head_masks()
    att, gq, gk, gv = [], [], [], []
    for p in range(pairs):
        keys, vals = lanes(kv, p), lanes(kv, pairs + p)
        q, g = lanes(query, p), lanes(grad_att, p)
        sums = None
        for mask in masks:
            qm, gm = masked(q, mask), masked(g, mask)
            prob = probabilities(qm, keys, bias)
            prob_b = prob.astype(bf16)
            dscore = score_gradient(prob, dot_nt(gm, vals))
            new = (
                dot(prob_b[:own], vals) * mask,
                dot(dscore[:own], keys) * mask,
                dot_tn(dscore[:, :PAIR], qm)[:own],
                dot_tn(prob_b[:, :PAIR], gm)[:own],
            )
            sums = new if sums is None else tuple(a + b for a, b in zip(sums, new))
        for group, part in zip((att, gq, gk, gv), sums):
            group.append(part.astype(bf16))
    attended = jnp.concatenate(att, axis=1)
    grad_proj = jnp.concatenate(gq + gk + gv, axis=1)
    grad_normed = dot_nt(grad_proj, w_qkv[...])
    grad_in, gain_part = norm_backward(values[:own], scale[:own], gain[...], grad_normed)
    gain_out[...] = gain_part
    c_b = (u_b[:own].astype(f32) + grad_in).astype(bf16)
    grad_merged_out[...] = dot_nt(c_b, w_merge[...])
    first = parity[0] == 0
    place = 0
    for x in (merged[...], normed[:own], attended):
        half = x.shape[1] // 2
        low, high = x[:, :half].astype(f32), x[:, half:].astype(f32)
        keep_out[:, place : place + half] = jnp.where(first, low, high).astype(bf16)
        send_out[:, place : place + half] = jnp.where(first, high, low).astype(bf16)
        place += half
    for g in (c_b, grad_proj, u_b[:own]):
        send_out[:, place : place + g.shape[1]] = g
        place += g.shape[1]


def coarse_weights_kernel(factor, keep, sent, got, out):
    half = keep.shape[1]
    width = half // 2
    x = jnp.concatenate([keep[...], got[:, :half]], axis=0)
    g = jnp.concatenate([sent[:, half:], got[:, half:]], axis=0)
    wide = x.shape[1] // 2
    narrow = wide // 2
    cols = width
    out[:wide] = (dot_tn(x[:, :wide], g[:, :cols]) * factor).astype(bf16)
    normed, attended = x[:, wide : wide + narrow], x[:, wide + narrow :]
    for b in range(3):
        rows = slice(wide + b * narrow, wide + (b + 1) * narrow)
        out[rows] = (dot_tn(normed, g[:, (b + 1) * cols : (b + 2) * cols]) * factor).astype(bf16)
    out[wide + 3 * narrow :] = (dot_tn(attended, g[:, 4 * cols :]) * factor).astype(bf16)


def fine_backward_kernel(
    grad_fine, grad_merged, perm, query_in, kv_in, w_out, band, valid,
    up_out, gq_out, mid_out, left_out, right_out,
):
    width = grad_fine.shape[1]
    pairs = width // PAIR
    total = jnp.concatenate([grad_merged[:, p * width : (p + 1) * width] for p in range(4)], axis=0)
    up = dot(perm[...], grad_fine[...]) + total
    up_out[...] = up
    grad_att = dot_nt(up.astype(bf16), w_out[...]).astype(bf16)
    query, kv = query_in[...], kv_in[...]
    bias = band[...] + valid[...]
    masks = head_masks()
    middle, side = mid_out.shape[0], left_out.shape[0]
    for p in range(pairs):
        keys, vals = lanes(kv, p), lanes(kv, pairs + p)
        q, g = lanes(query, p), lanes(grad_att, p)
        sums = None
        for mask in masks:
            qm, gm = masked(q, mask), masked(g, mask)
            prob = probabilities(qm, keys, bias)
            dscore = score_gradient(prob, dot_nt(gm, vals))
            new = (
                dot(dscore, keys) * mask,
                dot_tn(dscore, qm),
                dot_tn(prob.astype(bf16), gm),
            )
            sums = new if sums is None else tuple(a + b for a, b in zip(sums, new))
        gq_out[:, p * PAIR : (p + 1) * PAIR] = sums[0].astype(bf16)
        for part, at in ((sums[1], p), (sums[2], pairs + p)):
            where = slice(at * PAIR, (at + 1) * PAIR)
            mid_out[:, where] = part[:middle]
            left_out[:, where] = part[middle : middle + side].astype(bf16)
            right_out[:, where] = part[middle + side :].astype(bf16)


def fine_fold_kernel(mid, from_left, from_right, place_left, place_right, own_out, top_out, bottom_out):
    folded = mid[...] + dot(place_left[...], from_left[...]) + dot(place_right[...], from_right[...])
    own, rim = own_out.shape[0], top_out.shape[0]
    own_out[...] = folded[:own]
    top_out[...] = folded[own : own + rim].astype(bf16)
    bottom_out[...] = folded[own + rim :].astype(bf16)


def fine_last_kernel(
    own, from_above, from_below, place_above, place_below, gq, up, tok, perm, normed, att, gain, w_qkv, parity,
    grad_out, gain_out, keep_out, send_out,
):
    width = tok.shape[1]
    kv = own[...] + dot(place_above[...], from_above[...]) + dot(place_below[...], from_below[...])
    grad_proj = jnp.concatenate([gq[...], kv.astype(bf16)], axis=1)
    values, scale, _ = norm_forward(dot(perm[...], tok[...]), gain[...])
    grad_in, gain_part = norm_backward(values, scale, gain[...], dot_nt(grad_proj, w_qkv[...]))
    gain_out[...] = gain_part
    grad_out[...] = dot_tn(perm[...], (up[...] + grad_in).astype(bf16)).astype(bf16)
    first = parity[0] == 0
    half = width // 2
    place = 0
    for x in (normed[...], att[...]):
        low, high = x[:, :half].astype(f32), x[:, half:].astype(f32)
        keep_out[:, place : place + half] = jnp.where(first, low, high).astype(bf16)
        send_out[:, place : place + half] = jnp.where(first, high, low).astype(bf16)
        place += half
    send_out[:, place : place + 3 * width] = grad_proj
    send_out[:, place + 3 * width :] = up[...].astype(bf16)


def fine_weights_kernel(factor, keep, sent, got, out):
    wide = keep.shape[1]
    half = wide // 2
    x = jnp.concatenate([keep[...], got[:, :wide]], axis=0)
    g = jnp.concatenate([sent[:, wide:], got[:, wide:]], axis=0)
    qkv = (dot_tn(x[:, :half], g[:, : 3 * wide]) * factor).astype(bf16)
    last = (dot_tn(x[:, half:], g[:, 3 * wide :]) * factor).astype(bf16)
    out[:half] = qkv[:, : 2 * wide]
    out[half:, :wide] = qkv[:, 2 * wide :]
    out[half:, wide:] = last


def call(kernel, outs, flops=1 << 28):
    vmem = pl.BlockSpec(memory_space=pltpu.VMEM)
    smem = pl.BlockSpec(memory_space=pltpu.SMEM)

    def run(*args):
        return pl.pallas_call(
            kernel,
            out_shape=[jax.ShapeDtypeStruct(shape, dtype) for shape, dtype in outs],
            in_specs=[smem if a.ndim == 1 else vmem for a in args],
            out_specs=[vmem] * len(outs),
            compiler_params=pltpu.CompilerParams(vmem_limit_bytes=48 << 20),
            cost_estimate=pl.CostEstimate(flops=flops, bytes_accessed=4 << 20, transcendentals=0),
        )(*args)

    return run


def scatter_over_columns(x):
    count = lax.axis_size("col")
    pieces = lax.all_to_all(x, "col", 0, 0)
    return jnp.sum(pieces.reshape(count, -1, x.shape[-1]).astype(f32), axis=0).astype(bf16)


def reduce_rows(x, small):
    half = x.shape[0] // 2
    mine = (lax.axis_index("row") // 2) % 2
    keep = lax.dynamic_slice_in_dim(x, mine * half, half, axis=0)
    send = lax.dynamic_slice_in_dim(x, (1 - mine) * half, half, axis=0)
    got = flip(jnp.concatenate([send, small], axis=0), "row", 2)
    x = add_b(jnp.concatenate([keep, small], axis=0), got)
    bit = 4
    while bit < lax.axis_size("row"):
        x = add_b(x, flip(x, "row", bit))
        bit *= 2
    x, small = x[:half], x[half:]
    other = flip(x, "row", 2)
    return jnp.where(mine == 0, jnp.concatenate([x, other]), jnp.concatenate([other, x])), small


def per_device(
    tokens,
    gain_fine,
    qkv_fine,
    out_fine,
    w_merge,
    gain_coarse,
    qkv_coarse,
    out_coarse,
    grad_fine,
    grad_coarse,
):
    rows, columns, width = tokens.shape
    crows, ccolumns, cwidth = grad_coarse.shape
    reach = RADIUS
    count, ccount = rows * columns, crows * ccolumns
    parity = (lax.axis_index("row") % 2).astype(jnp.int32)[None]
    factor = 1.0 / math.sqrt(rows * lax.axis_size("row") * columns * lax.axis_size("col"))
    tok = tokens.reshape(count, width)
    gc = grad_coarse.reshape(ccount, cwidth)

    rim, crim = reach * columns, reach * ccolumns

    def pack(a, b):
        return jnp.concatenate([a, b[:, :width], b[:, width:]], axis=0)

    def unpack(x, n):
        m = n + (x.shape[0] - n) // 2
        return x[:n], jnp.concatenate([x[n:m], x[m:]], axis=1)

    top, ctop = unpack(shifted(pack(tok[-rim:], gc[-crim:]), "row", 1), rim)
    bottom, cbottom = unpack(shifted(pack(tok[:rim], gc[:crim]), "row", -1), rim)
    tall = jnp.concatenate([top, tok, bottom], axis=0).reshape(-1, columns, width)
    ctall = jnp.concatenate([ctop, gc, cbottom], axis=0).reshape(-1, ccolumns, cwidth)
    keys0 = fine_keys(rows, columns)
    side = len(keys0[3])
    queries1 = coarse_queries(crows, ccolumns)
    cside = len(queries1[3])

    def edge(x, start, stop, length):
        flat = x[:, start:stop].reshape(-1, x.shape[-1])
        return jnp.pad(flat, ((0, length - flat.shape[0]), (0, 0)))

    left, cleft = unpack(
        shifted(
            pack(
                edge(tall, columns - reach, columns, side),
                edge(ctall, ccolumns - reach, ccolumns, cside),
            ),
            "col",
            1,
        ),
        side,
    )
    right, cright = unpack(
        shifted(pack(edge(tall, 0, reach, side), edge(ctall, 0, reach, cside)), "col", -1), side
    )
    upstream1 = jnp.concatenate([gc, ctop, cbottom, cleft, cright], axis=0)

    flat0 = joined(keys0)
    own0 = keys0[0]
    natural = grid_piece(range(rows), range(columns))
    perm = jnp.asarray(one_hot(own0, natural))
    band0 = jnp.asarray(band_bias(own0, flat0))
    valid0 = key_bias(flat0, rows, columns)
    gain0, gain1 = gain_fine[None, :], gain_coarse[None, :]
    merged, coarse_in, normed0, query0, kv0, att0 = call(
        fine_forward_kernel,
        [
            ((ccount, 4 * width), bf16),
            ((ccount, cwidth), bf16),
            ((count, width), bf16),
            ((count, width), bf16),
            ((len(flat0), 2 * width), bf16),
            ((count, width), bf16),
        ],
    )(tok, top, bottom, left, right, perm, gain0, qkv_fine, out_fine, w_merge, band0, valid0)

    wide = 2 * reach
    part = (wide - crows) * ccolumns
    up1 = shifted(coarse_in, "row", 1)
    up2 = shifted(coarse_in[-part:], "row", 2)
    down1 = shifted(coarse_in, "row", -1)
    down2 = shifted(coarse_in[:part], "row", -2)
    tall = jnp.concatenate([up2, up1, coarse_in, down1, down2], axis=0)
    tall = tall.reshape(-1, ccolumns, cwidth)
    cl = shifted(tall[:, ccolumns - wide :].reshape(-1, cwidth), "col", 1)
    cr = shifted(tall[:, :wide].reshape(-1, cwidth), "col", -1)
    field = jnp.concatenate([coarse_in, up1, down1, up2, down2, cl, cr], axis=0)

    flat1, ask1 = joined(coarse_keys(crows, ccolumns)), joined(queries1)
    band1 = jnp.asarray(band_bias(ask1, flat1))
    valid1 = key_bias(flat1, crows, ccolumns)
    pick = jnp.asarray(one_hot(ask1, flat1))
    kept = (4 * width + 2 * cwidth) // 2
    keep1, send1, gain_part1, grad_merged = call(
        coarse_kernel,
        [
            ((ccount, kept), bf16),
            ((ccount, kept + 5 * cwidth), bf16),
            ((1, cwidth), f32),
            ((ccount, 4 * width), f32),
        ],
    )(field, upstream1, merged, pick, gain1, qkv_coarse, out_coarse, w_merge, band1, valid1, parity)
    (packed1,) = call(
        functools.partial(coarse_weights_kernel, factor),
        [((2 * width + 4 * cwidth // 2, cwidth), bf16)],
    )(keep1, send1, flip(send1, "row", 1))
    cols = lax.axis_size("col")
    sums1 = scatter_over_columns(packed1.reshape(cols, -1, cwidth))

    rims = len(keys0[1])
    middle = count + 2 * rims
    up0, gq0, mid, left_rim, right_rim = call(
        fine_backward_kernel,
        [
            ((count, width), f32),
            ((count, width), bf16),
            ((middle, 2 * width), f32),
            ((side, 2 * width), bf16),
            ((side, 2 * width), bf16),
        ],
    )(grad_fine.reshape(count, width), grad_merged, perm, query0, kv0, out_fine, band0, valid0)
    from_right = shifted(left_rim, "col", -1)
    from_left = shifted(right_rim, "col", 1)
    mids = joined(keys0[:3])

    def moved(piece, dr, dc):
        return [None if p is None else (p[0] + dr, p[1] + dc) for p in piece]

    own, top_rim, bottom_rim = call(
        fine_fold_kernel,
        [((count, 2 * width), f32), ((rims, 2 * width), bf16), ((rims, 2 * width), bf16)],
    )(
        mid,
        from_left,
        from_right,
        jnp.asarray(one_hot(mids, moved(keys0[4], 0, -columns))),
        jnp.asarray(one_hot(mids, moved(keys0[3], 0, columns))),
    )
    from_below = shifted(top_rim, "row", -1)
    from_above = shifted(bottom_rim, "row", 1)
    grad_tokens, gain_part0, keep0, send0 = call(
        fine_last_kernel,
        [
            ((count, width), bf16),
            ((1, width), f32),
            ((count, width), bf16),
            ((count, 5 * width), bf16),
        ],
    )(
        own,
        from_above,
        from_below,
        jnp.asarray(one_hot(own0, moved(keys0[2], -rows, 0))),
        jnp.asarray(one_hot(own0, moved(keys0[1], rows, 0))),
        gq0,
        up0,
        tok,
        perm,
        normed0,
        att0,
        gain0,
        qkv_fine,
        parity,
    )
    (packed0,) = call(
        functools.partial(fine_weights_kernel, factor), [((width, 2 * width), bf16)]
    )(keep0, send0, flip(send0, "row", 1))
    gains = jnp.concatenate([gain_part0[0], gain_part1[0]]) * factor
    gains = jnp.pad(gains, (0, 16 * cwidth - gains.shape[0])).reshape(16, cwidth).astype(bf16)
    pieces0 = packed0.reshape(cols, -1, cwidth)
    pieces0 = jnp.concatenate([pieces0, jnp.broadcast_to(gains, (cols, 16, cwidth))], axis=1)
    sums0 = scatter_over_columns(pieces0)

    n1, n0 = sums1.shape[0], sums0.shape[0] - 16
    x, small = reduce_rows(jnp.concatenate([sums1, sums0[:n0]], axis=0), sums0[n0:])
    x = lax.all_to_all(jnp.broadcast_to(x, (cols,) + x.shape), "col", 0, 0).reshape(-1, cwidth)
    got = flip(jnp.concatenate([x, small], axis=0), "row", 1)
    other = got[: x.shape[0]]
    gains = (small.astype(f32) + got[x.shape[0] :].astype(f32)).reshape(-1)
    first = parity[0] == 0

    def halves(start, stop, place, length):
        def take(a):
            block = a.reshape(cols, n1 + n0, cwidth)[:, start:stop].reshape(-1, cwidth)
            return block[place : place + length]

        mine, others = take(x), take(other)
        return jnp.where(first, mine, others), jnp.where(first, others, mine)

    def whole(start, stop, place, length):
        return jnp.concatenate(halves(start, stop, place, length), axis=0)

    half = cwidth // 2
    grad_merge = whole(0, n1, 0, 2 * width)
    blocks = [whole(0, n1, 2 * width + b * half, half) for b in range(4)]
    low = whole(n1, n1 + n0, 0, width // 2)
    high = whole(n1, n1 + n0, width // 2, width // 2)
    return (
        grad_tokens.reshape(rows, columns, width),
        gains[:width],
        jnp.concatenate([low, high[:, :width]], axis=1),
        high[:, width:],
        grad_merge,
        gains[width : width + cwidth],
        jnp.concatenate(blocks[:3], axis=1),
        blocks[3],
    )


def solution(mesh):
    in_specs = (
        P("row", "col", None),
        P(),
        P(),
        P(),
        P(),
        P(),
        P(),
        P(),
        P("row", "col", None),
        P("row", "col", None),
    )
    out_specs = (P("row", "col", None), P(), P(), P(), P(), P(), P(), P())
    return jax.shard_map(
        per_device, mesh=mesh, in_specs=in_specs, out_specs=out_specs, check_vma=False
    )
```

```python
import functools
import math

import jax
import jax.numpy as jnp
import numpy as np
from jax import lax
from jax.experimental import pallas as pl
from jax.experimental.pallas import tpu as pltpu
from jax.sharding import PartitionSpec as P

HEAD = 64
RADIUS = 3
PAIR = 2 * HEAD
TILE = (8, 16)
VMEM = 32 << 20
NEG = -1e30
norm_eps = 1e-06
f32 = jnp.float32
bf16 = jnp.bfloat16


def shifted(x, axis, by):
    count = lax.axis_size(axis)
    pairs = [(i, i + by) for i in range(count) if 0 <= i + by < count]
    return lax.ppermute(x, axis, pairs)


def flip(x, axis, bit):
    return lax.ppermute(x, axis, [(i, i ^ bit) for i in range(lax.axis_size(axis))])


def add_b(a, b):
    return (a.astype(f32) + b.astype(f32)).astype(bf16)


def grid_piece(rows, columns, length=None):
    piece = [(r, c) for r in rows for c in columns]
    return piece + [None] * ((length or len(piece)) - len(piece))


def merge_order(rows, columns):
    return [
        (2 * a + rp, 2 * b + cp)
        for rp in (0, 1)
        for cp in (0, 1)
        for a in range(rows // 2)
        for b in range(columns // 2)
    ]


def fine_keys(rows, columns):
    near, reach = RADIUS + 1, 2 * RADIUS + 1
    tall = range(-reach, rows + reach)
    side = -(-len(tall) * RADIUS // 16) * 16
    rim = merge_order(near, columns)
    return [
        merge_order(rows, columns),
        [(r - near, c) for r, c in rim],
        [(r + rows, c) for r, c in rim],
        grid_piece(range(-reach, -near), range(columns)),
        grid_piece(range(rows + near, rows + reach), range(columns)),
        grid_piece(tall, range(-RADIUS, 0), side),
        grid_piece(tall, range(columns, columns + RADIUS), side),
    ]


def back_keys(rows, columns):
    tall = range(-RADIUS, rows + RADIUS)
    side = -(-len(tall) * RADIUS // 16) * 16
    return [
        merge_order(rows, columns),
        grid_piece(range(-RADIUS, 0), range(columns)),
        grid_piece(range(rows, rows + RADIUS), range(columns)),
        grid_piece(tall, range(-RADIUS, 0), side),
        grid_piece(tall, range(columns, columns + RADIUS), side),
    ]


def coarse_keys(rows, columns):
    reach = 2 * RADIUS
    tall = range(-reach, rows + reach)
    return [
        grid_piece(range(rows), range(columns)),
        grid_piece(range(-2, 0), range(columns)),
        grid_piece(range(rows, rows + 2), range(columns)),
        grid_piece(range(-reach, -2), range(columns)),
        grid_piece(range(rows + 2, rows + reach), range(columns)),
        grid_piece(tall, range(-reach, 0)),
        grid_piece(tall, range(columns, columns + reach)),
    ]


def coarse_queries(rows, columns):
    reach = RADIUS
    tall = range(-reach, rows + reach)
    side = -(-len(tall) * reach // 16) * 16
    return [
        grid_piece(range(rows), range(columns)),
        grid_piece(range(-reach, 0), range(columns)),
        grid_piece(range(rows, rows + reach), range(columns)),
        grid_piece(tall, range(-reach, 0), side),
        grid_piece(tall, range(columns, columns + reach), side),
    ]


def joined(pieces):
    return [place for piece in pieces for place in piece]


def band_bias(queries, keys):
    bias = np.full((len(queries), len(keys)), NEG, np.float32)
    for i, q in enumerate(queries):
        for j, k in enumerate(keys):
            if q is None:
                inside = j == 0
            else:
                inside = k is not None and max(abs(q[0] - k[0]), abs(q[1] - k[1])) <= RADIUS
            if inside:
                bias[i, j] = 0.0
    return bias


def places(keys):
    return Late(jnp.asarray(np.array([[k[i] if k else 0 for k in keys] for i in (0, 1)], np.int32)))


def one_hot(targets, sources):
    place = {s: j for j, s in enumerate(sources) if s is not None}
    matrix = np.zeros((len(targets), len(sources)), np.float32)
    for i, t in enumerate(targets):
        if t is not None and t in place:
            matrix[i, place[t]] = 1.0
    return matrix.astype(jnp.bfloat16)


def dot(a, b):
    return jnp.dot(a, b, preferred_element_type=f32)


def dot_nt(a, b):
    return lax.dot_general(a, b, (((1,), (1,)), ((), ())), preferred_element_type=f32)


def dot_tn(a, b):
    return lax.dot_general(a, b, (((0,), (0,)), ((), ())), preferred_element_type=f32)


def norm_forward(x, gain):
    values = x.astype(f32)
    scale = lax.rsqrt(jnp.mean(values * values, axis=-1, keepdims=True) + norm_eps)
    return values, scale, (values * scale * gain).astype(bf16)


def norm_backward(values, scale, gain, upstream):
    gain_part = jnp.sum(upstream * values * scale, axis=0, keepdims=True)
    weighted = upstream * gain
    inner = jnp.mean(weighted * values, axis=-1, keepdims=True)
    return weighted * scale - values * (scale * scale * scale) * inner, gain_part


def validity(at, where, rows, columns):
    row = at[0:1, :] + where[0] * rows
    col = at[1:2, :] + where[1] * columns
    ok = (row >= 0) & (row < where[2] * rows) & (col >= 0) & (col < where[3] * columns)
    return jnp.where(ok, 0.0, NEG)


def split_rows(x):
    half = x.shape[1] // 2
    return jnp.concatenate([x[:, :half], x[:, half:]], axis=0)


def join_rows(x):
    half = x.shape[0] // 2
    return jnp.concatenate([x[:half], x[half:]], axis=1)


def head_masks():
    lane = lax.broadcasted_iota(jnp.int32, (1, PAIR), 1)
    return [(lane < HEAD).astype(f32), (lane >= HEAD).astype(f32)]


def masked(x, mask):
    return (x.astype(f32) * mask).astype(bf16)


def probabilities(query, keys, bias):
    weights = jnp.exp(dot_nt(query, keys) * (1.0 / math.sqrt(HEAD)) + bias)
    total = jnp.sum(weights, axis=-1, keepdims=True)
    return weights / jnp.where(total > 0.0, total, 1.0)


def score_gradient(prob, dprob):
    total = jnp.sum(prob * dprob, axis=-1, keepdims=True)
    return (prob * (dprob - total) * (1.0 / math.sqrt(HEAD))).astype(bf16)


def lanes(x, place):
    return x[:, place * PAIR : (place + 1) * PAIR]


def rows_pack_kernel(tok, gc, down_out, up_out):
    rim = down_out.shape[0] - 2 * gc.shape[0]
    both = split_rows(gc[...])
    down_out[:rim] = tok[tok.shape[0] - rim :, :]
    up_out[:rim] = tok[:rim, :]
    down_out[rim:] = both
    up_out[rim:] = both


def columns_pack_kernel(tok, gc, up, down, pick, cpick, right_out, left_out):
    rim = up.shape[0] - 2 * gc.shape[0]
    side = pick.shape[0] // 2
    cside = cpick.shape[0] // 2
    field = jnp.concatenate([tok[...], up[:rim], down[:rim]], axis=0)
    sends = dot(pick[...], field).astype(bf16)
    coarse = jnp.concatenate([gc[...], join_rows(up[rim:]), join_rows(down[rim:])], axis=0)
    csends = dot(cpick[...], coarse).astype(bf16)
    right_out[:side] = sends[:side]
    left_out[:side] = sends[side:]
    right_out[side:] = split_rows(csends[:cside])
    left_out[side:] = split_rows(csends[cside:])


def coarse_pack_kernel(near, up, down, pick, right_out, left_out):
    field = jnp.concatenate([near[...], up[...], down[...]], axis=0)
    sends = dot(pick[...], field).astype(bf16)
    side = right_out.shape[0]
    right_out[...] = sends[:side]
    left_out[...] = sends[side:]


def fine_forward_kernel(
    tok, up, down, left, right, perm, perm_rim, gain, w_qkv, w_out, w_merge, band, at, where,
    merged_out, near_out, down_out, up_out, normed_out, proj_out, kv_out, att_out,
):
    width = tok.shape[1]
    count, rim = perm.shape[0], perm_rim.shape[0]
    far = up.shape[0] - 2 * merged_out.shape[0]
    side = (kv_out.shape[0] - count - 2 * far) // 2
    own = dot(perm[...], tok[...]).astype(bf16)
    above = dot(perm_rim[...], up[far - rim : far]).astype(bf16)
    below = dot(perm_rim[...], down[:rim]).astype(bf16)
    inner = jnp.concatenate([own, above, below], axis=0)
    field = jnp.concatenate(
        [inner, up[: far - rim], down[rim:far], left[:side], right[:side]], axis=0
    )
    _, _, normed = norm_forward(field, gain[...])
    normed_out[...] = normed[:count]
    asked = inner.shape[0]
    query = dot(normed[:asked], w_qkv[:, :width]).astype(bf16)
    kv = dot(normed, w_qkv[:, width:]).astype(bf16)
    proj_out[...] = query[:count]
    kv_out[...] = kv
    bias = band[...] + validity(at[...], where, *TILE)
    masks = head_masks()
    parts = []
    for p in range(width // PAIR):
        keys, vals, q = lanes(kv, p), lanes(kv, width // PAIR + p), lanes(query, p)
        total = None
        for mask in masks:
            prob = probabilities(masked(q, mask), keys, bias)
            part = dot(prob.astype(bf16), vals) * mask
            total = part if total is None else total + part
        parts.append(total.astype(bf16))
    attended = jnp.concatenate(parts, axis=1)
    att_out[...] = attended[:count]
    fine = (inner.astype(f32) + dot(attended, w_out[...])).astype(bf16)
    quarter, small = count // 4, rim // 4
    acc = None
    for p in range(4):
        block = fine[p * quarter : (p + 1) * quarter]
        merged_out[:, p * width : (p + 1) * width] = block
        upper = fine[count + p * small : count + (p + 1) * small]
        lower = fine[count + rim + p * small : count + rim + (p + 1) * small]
        block = jnp.concatenate([block, upper, lower], axis=0)
        part = dot(block, w_merge[p * width : (p + 1) * width, :])
        acc = part if acc is None else acc + part
    near = acc.astype(bf16)
    near_out[...] = near
    half = quarter // 2
    down_out[:small] = near[quarter : quarter + small]
    down_out[small:] = near[:half]
    up_out[:half] = near[half:quarter]
    up_out[half:] = near[quarter + small :]


def coarse_kernel(
    near, up, down, left, right, gc, gup, gdown, gleft, gright, merged, pick, gpick,
    gain, w_qkv, w_out, w_merge, band, at, where,
    keep_out, send_out, gain_out, grad_merged_out,
):
    own, width = merged.shape[0], near.shape[1]
    pairs = width // PAIR
    field = jnp.concatenate([near[...], up[...], down[...], left[...], right[...]], axis=0)
    values, scale, normed = norm_forward(field, gain[...])
    kv = dot(normed, w_qkv[:, width:]).astype(bf16)
    picked = dot(pick[...], normed).astype(bf16)
    query = dot(picked, w_qkv[:, :width]).astype(bf16)
    tall, wide = gup.shape[0] - 2 * own, gleft.shape[0] - 2 * (gpick.shape[1] - 3 * own) // 2
    given = [gc[...], join_rows(gup[tall:]), join_rows(gdown[tall:])]
    given += [join_rows(gleft[wide:]), join_rows(gright[wide:])]
    u_b = dot(gpick[...], jnp.concatenate(given, axis=0)).astype(bf16)
    grad_att = dot_nt(u_b, w_out[...]).astype(bf16)
    bias = band[...] + validity(at[...], where, TILE[0] // 2, TILE[1] // 2)
    masks = head_masks()
    att, gq, gk, gv = [], [], [], []
    for p in range(pairs):
        keys, vals = lanes(kv, p), lanes(kv, pairs + p)
        q, g = lanes(query, p), lanes(grad_att, p)
        sums = None
        for mask in masks:
            qm, gm = masked(q, mask), masked(g, mask)
            prob = probabilities(qm, keys, bias)
            prob_b = prob.astype(bf16)
            dscore = score_gradient(prob, dot_nt(gm, vals))
            new = (
                dot(prob_b[:own], vals) * mask,
                dot(dscore[:own], keys) * mask,
                dot_tn(dscore[:, :PAIR], qm)[:own],
                dot_tn(prob_b[:, :PAIR], gm)[:own],
            )
            sums = new if sums is None else tuple(a + b for a, b in zip(sums, new))
        for group, part in zip((att, gq, gk, gv), sums):
            group.append(part.astype(bf16))
    attended = jnp.concatenate(att, axis=1)
    grad_proj = jnp.concatenate(gq + gk + gv, axis=1)
    grad_normed = dot_nt(grad_proj, w_qkv[...])
    grad_in, gain_part = norm_backward(values[:own], scale[:own], gain[...], grad_normed)
    gain_out[...] = gain_part
    c_b = (u_b[:own].astype(f32) + grad_in).astype(bf16)
    grad_merged_out[...] = dot_nt(c_b, w_merge[...])
    first = where[0] % 2 == 0
    place = 0
    for x in (merged[...], normed[:own], attended):
        half = x.shape[1] // 2
        low, high = x[:, :half].astype(f32), x[:, half:].astype(f32)
        keep_out[:, place : place + half] = jnp.where(first, low, high).astype(bf16)
        send_out[:, place : place + half] = jnp.where(first, high, low).astype(bf16)
        place += half
    for g in (c_b, grad_proj, u_b[:own]):
        send_out[:, place : place + g.shape[1]] = g
        place += g.shape[1]


def coarse_weights_kernel(factor, keep, sent, got, out):
    half = keep.shape[1]
    cols = out.shape[2]
    x = jnp.concatenate([keep[...], got[:, :half]], axis=0)
    g = jnp.concatenate([sent[:, half:], got[:, half:]], axis=0)
    wide = half // 2
    narrow = wide // 2
    normed, attended = x[:, wide : wide + narrow], x[:, wide + narrow :]
    parts = [(x[:, :wide], 0)] + [(normed, b) for b in (1, 2, 3)] + [(attended, 4)]
    place = 0
    for a, b in parts:
        part = (dot_tn(a, g[:, b * cols : (b + 1) * cols]) * factor).astype(bf16)
        rows = part.shape[0] // out.shape[0]
        for j in range(out.shape[0]):
            out[j, place : place + rows] = part[j * rows : (j + 1) * rows]
        place += rows


def fine_backward_kernel(
    grad_fine, grad_merged, perm, query_in, kv_in, pick, w_out, band, at, where,
    up_out, gq_out, mid_out, left_out, right_out,
):
    width = grad_fine.shape[1]
    pairs = width // PAIR
    total = jnp.concatenate([grad_merged[:, p * width : (p + 1) * width] for p in range(4)], axis=0)
    up = dot(perm[...], grad_fine[...]) + total
    up_out[...] = up
    grad_att = dot_nt(up.astype(bf16), w_out[...]).astype(bf16)
    query = query_in[...]
    kv = dot(pick[...], kv_in[...]).astype(bf16)
    bias = band[...] + validity(at[...], where, *TILE)
    masks = head_masks()
    middle, side = mid_out.shape[0], left_out.shape[0]
    for p in range(pairs):
        keys, vals = lanes(kv, p), lanes(kv, pairs + p)
        q, g = lanes(query, p), lanes(grad_att, p)
        sums = None
        for mask in masks:
            qm, gm = masked(q, mask), masked(g, mask)
            prob = probabilities(qm, keys, bias)
            dscore = score_gradient(prob, dot_nt(gm, vals))
            new = (
                dot(dscore, keys) * mask,
                dot_tn(dscore, qm),
                dot_tn(prob.astype(bf16), gm),
            )
            sums = new if sums is None else tuple(a + b for a, b in zip(sums, new))
        gq_out[:, p * PAIR : (p + 1) * PAIR] = sums[0].astype(bf16)
        for part, at in ((sums[1], p), (sums[2], pairs + p)):
            where = slice(at * PAIR, (at + 1) * PAIR)
            mid_out[:, where] = part[:middle]
            left_out[:, where] = part[middle : middle + side].astype(bf16)
            right_out[:, where] = part[middle + side :].astype(bf16)


def fine_fold_kernel(mid, from_left, from_right, place_left, place_right, own_out, top_out, bottom_out):
    folded = mid[...] + dot(place_left[...], from_left[...]) + dot(place_right[...], from_right[...])
    own, rim = own_out.shape[0], top_out.shape[0]
    own_out[...] = folded[:own]
    top_out[...] = folded[own : own + rim].astype(bf16)
    bottom_out[...] = folded[own + rim :].astype(bf16)


def fine_last_kernel(
    own, from_above, from_below, place_above, place_below, gq, up, tok, perm, normed, att, gain, w_qkv, where,
    grad_out, gain_out, keep_out, send_out,
):
    width = tok.shape[1]
    kv = own[...] + dot(place_above[...], from_above[...]) + dot(place_below[...], from_below[...])
    grad_proj = jnp.concatenate([gq[...], kv.astype(bf16)], axis=1)
    values, scale, _ = norm_forward(dot(perm[...], tok[...]), gain[...])
    grad_in, gain_part = norm_backward(values, scale, gain[...], dot_nt(grad_proj, w_qkv[...]))
    gain_out[...] = gain_part
    grad_out[...] = dot_tn(perm[...], (up[...] + grad_in).astype(bf16)).astype(bf16)
    first = where[0] % 2 == 0
    half = width // 2
    place = 0
    for x in (normed[...], att[...]):
        low, high = x[:, :half].astype(f32), x[:, half:].astype(f32)
        keep_out[:, place : place + half] = jnp.where(first, low, high).astype(bf16)
        send_out[:, place : place + half] = jnp.where(first, high, low).astype(bf16)
        place += half
    send_out[:, place : place + 3 * width] = grad_proj
    send_out[:, place + 3 * width :] = up[...].astype(bf16)


def fine_weights_kernel(factor, keep, sent, got, gain, cgain, out):
    wide = keep.shape[1]
    half = wide // 2
    x = jnp.concatenate([keep[...], got[:, :wide]], axis=0)
    g = jnp.concatenate([sent[:, wide:], got[:, wide:]], axis=0)
    qkv = (dot_tn(x[:, :half], g[:, : 3 * wide]) * factor).astype(bf16)
    last = (dot_tn(x[:, half:], g[:, 3 * wide :]) * factor).astype(bf16)
    rows = half // out.shape[0]
    zeros = jnp.zeros((14, 2 * wide), f32)
    padded = jnp.concatenate([gain[...], jnp.zeros((1, wide), f32)], axis=1)
    gains = jnp.concatenate([cgain[...], padded, zeros], axis=0)
    gains = (gains * factor).astype(bf16)
    for j in range(out.shape[0]):
        at = slice(j * rows, (j + 1) * rows)
        out[j, :rows] = qkv[at, : 2 * wide]
        out[j, rows : 2 * rows, :wide] = qkv[at, 2 * wide :]
        out[j, rows : 2 * rows, wide:] = last[at]
        out[j, 2 * rows :] = gains


def unpack_kernel(where, mine, other, merge, qkv1, out1, qkv0, out0, *scratch):
    first = where[0] % 2
    cols, width = mine.shape[0], mine.shape[2]
    half = width // 2
    sems = scratch[-1]
    outs = (merge, qkv1, out1, qkv0, out0)
    m, q1, o1, q0, o0 = scratch[:-1]
    at = 0
    copies = []

    def move(rows, lanes, dst, dst_lanes):
        for src, core in ((mine, first), (other, 1 - first)):
            for j in range(cols):
                dst[core * cols + j, :, dst_lanes] = src[j, rows, lanes]

    def finish(n):
        copies.append(pltpu.make_async_copy(scratch[n], outs[n], sems.at[n]))
        copies[-1].start()

    every = slice(0, width)
    for n in (0, 1, 2):
        rows = outs[n].shape[1]
        for b in range(outs[n].shape[2] // width):
            move(slice(at, at + rows), every, scratch[n], slice(b * width, (b + 1) * width))
            at += rows
        finish(n)
    rows = qkv0.shape[1]
    move(slice(at, at + rows), every, q0, every)
    at += rows
    move(slice(at, at + rows), slice(0, half), q0, slice(width, width + half))
    finish(3)
    move(slice(at, at + rows), slice(half, width), o0, slice(0, half))
    finish(4)
    for copy in copies:
        copy.wait()


class Late:
    def __init__(self, value):
        self.value = value


class Arriving:
    def __init__(self, ref, copy):
        self.ref, self.copy, self.shape = ref, copy, ref.shape

    def __getitem__(self, index):
        if self.copy is not None:
            self.copy.wait()
            self.copy = None
        return self.ref[index]


def call(kernel, outs, flops=1 << 28):
    vmem = pl.BlockSpec(memory_space=pltpu.VMEM)
    smem = pl.BlockSpec(memory_space=pltpu.SMEM)
    anywhere = pl.BlockSpec(memory_space=pl.ANY)

    def run(*args):
        late = [i for i, a in enumerate(args) if isinstance(a, Late)]
        given = [
            pltpu.with_memory_space_constraint(a.value, pltpu.HBM) if isinstance(a, Late) else a
            for a in args
        ]

        def body(*refs):
            ins, results = list(refs[: len(args)]), refs[len(args) : len(args) + len(outs)]
            rest = refs[len(args) + len(outs) :]
            arriving = []
            for n, i in enumerate(late):
                copy = pltpu.make_async_copy(ins[i], rest[n], rest[-1].at[n])
                copy.start()
                ins[i] = Arriving(rest[n], copy)
                arriving.append(ins[i])
            kernel(*ins, *results)
            for operand in arriving:
                if operand.copy is not None:
                    operand.copy.wait()

        scratch = [pltpu.VMEM(given[i].shape, given[i].dtype) for i in late]
        if late:
            scratch.append(pltpu.SemaphoreType.DMA((len(late),)))
        return pl.pallas_call(
            body,
            out_shape=[jax.ShapeDtypeStruct(shape, dtype) for shape, dtype in outs],
            in_specs=[
                anywhere if i in late else smem if a.ndim == 1 else vmem
                for i, a in enumerate(given)
            ],
            out_specs=[vmem] * len(outs),
            scratch_shapes=scratch,
            compiler_params=pltpu.CompilerParams(vmem_limit_bytes=VMEM),
            cost_estimate=pl.CostEstimate(flops=flops, bytes_accessed=4 << 20, transcendentals=0),
        )(*given)

    return run


def scatter_over_columns(x):
    count = lax.axis_size("col")
    pieces = lax.all_to_all(x, "col", 0, 0)
    return jnp.sum(pieces.reshape(count, -1, x.shape[-1]).astype(f32), axis=0).astype(bf16)


def reduce_rows(x, small):
    half = x.shape[0] // 2
    mine = (lax.axis_index("row") // 2) % 2
    keep = lax.dynamic_slice_in_dim(x, mine * half, half, axis=0)
    send = lax.dynamic_slice_in_dim(x, (1 - mine) * half, half, axis=0)
    got = flip(jnp.concatenate([send, small], axis=0), "row", 2)
    x = add_b(jnp.concatenate([keep, small], axis=0), got)
    bit = 4
    while bit < lax.axis_size("row"):
        x = add_b(x, flip(x, "row", bit))
        bit *= 2
    x, small = x[:half], x[half:]
    other = flip(x, "row", 2)
    return jnp.where(mine == 0, jnp.concatenate([x, other]), jnp.concatenate([other, x])), small


def per_device(
    tokens,
    gain_fine,
    qkv_fine,
    out_fine,
    w_merge,
    gain_coarse,
    qkv_coarse,
    out_coarse,
    grad_fine,
    grad_coarse,
):
    rows, columns, width = tokens.shape
    crows, ccolumns, cwidth = grad_coarse.shape
    count, ccount = rows * columns, crows * ccolumns
    cols = lax.axis_size("col")
    where = jnp.stack(
        [lax.axis_index("row"), lax.axis_index("col"), lax.axis_size("row"), cols]
    ).astype(jnp.int32)
    factor = 1.0 / math.sqrt(rows * lax.axis_size("row") * columns * cols)
    tok = Late(tokens.reshape(count, width))
    gc = Late(grad_coarse.reshape(ccount, cwidth))
    gain0, gain1 = Late(gain_fine[None, :]), Late(gain_coarse[None, :])
    qkv_fine, out_fine, w_merge = Late(qkv_fine), Late(out_fine), Late(w_merge)
    qkv_coarse, out_coarse = Late(qkv_coarse), Late(out_coarse)

    def moved(piece, dr, dc):
        return [None if p is None else (p[0] + dr, p[1] + dc) for p in piece]

    def chosen(targets, sources):
        return Late(jnp.asarray(one_hot(targets, sources)))

    keys0, keys1 = fine_keys(rows, columns), coarse_keys(crows, ccolumns)
    queries1 = coarse_queries(crows, ccolumns)
    natural = grid_piece(range(rows), range(columns))
    cnatural = queries1[0]
    rim = (2 * RADIUS + 1) * columns
    side, cside = len(keys0[5]), len(queries1[3])
    send_down, send_up = call(
        rows_pack_kernel, [((rim + 2 * ccount, width), bf16)] * 2, flops=1 << 20
    )(tok, gc)
    up = shifted(send_down, "row", 1)
    down = shifted(send_up, "row", -1)
    held = natural + moved(natural[-rim:], -rows, 0) + moved(natural[:rim], rows, 0)
    cheld = cnatural + moved(cnatural, -crows, 0) + moved(cnatural, crows, 0)
    send_right, send_left = call(
        columns_pack_kernel, [((side + 2 * cside, width), bf16)] * 2, flops=1 << 20
    )(
        tok,
        gc,
        up,
        down,
        chosen(moved(keys0[5], 0, columns) + moved(keys0[6], 0, -columns), held),
        chosen(moved(queries1[3], 0, ccolumns) + moved(queries1[4], 0, -ccolumns), cheld),
    )
    left = shifted(send_right, "col", 1)
    right = shifted(send_left, "col", -1)

    flat0 = joined(keys0)
    own0 = keys0[0]
    asked0 = joined(keys0[:3])
    perm = chosen(own0, natural)
    near = len(keys0[1])
    merged, near1, down1, up1, normed0, query0, kv0, att0 = call(
        fine_forward_kernel,
        [
            ((ccount, 4 * width), bf16),
            ((ccount + near // 2, cwidth), bf16),
            ((ccount, cwidth), bf16),
            ((ccount, cwidth), bf16),
            ((count, width), bf16),
            ((count, width), bf16),
            ((len(flat0), 2 * width), bf16),
            ((count, width), bf16),
        ],
    )(
        tok,
        up,
        down,
        left,
        right,
        perm,
        chosen(merge_order(RADIUS + 1, columns), natural[:near]),
        gain0,
        qkv_fine,
        out_fine,
        w_merge,
        Late(jnp.asarray(band_bias(asked0, flat0))),
        places(flat0),
        where,
    )

    above1 = shifted(down1, "row", 1)
    below1 = shifted(up1, "row", -1)
    tall1 = joined(keys1[:5])
    wide1 = len(keys1[5])
    send_right, send_left = call(
        coarse_pack_kernel, [((wide1, cwidth), bf16)] * 2, flops=1 << 20
    )(
        near1,
        above1,
        below1,
        chosen(moved(keys1[5], 0, ccolumns) + moved(keys1[6], 0, -ccolumns), tall1),
    )
    left1 = shifted(send_right, "col", 1)
    right1 = shifted(send_left, "col", -1)

    flat1, ask1 = joined(keys1), joined(queries1)
    kept = (4 * width + 2 * cwidth) // 2
    keep1, send1, gain_part1, grad_merged = call(
        coarse_kernel,
        [
            ((ccount, kept), bf16),
            ((ccount, kept + 5 * cwidth), bf16),
            ((1, cwidth), f32),
            ((ccount, 4 * width), f32),
        ],
    )(
        near1,
        above1,
        below1,
        left1,
        right1,
        gc,
        up,
        down,
        left,
        right,
        merged,
        chosen(ask1, flat1),
        chosen(ask1, cheld + queries1[3] + queries1[4]),
        gain1,
        qkv_coarse,
        out_coarse,
        w_merge,
        Late(jnp.asarray(band_bias(ask1, flat1))),
        places(flat1),
        where,
    )
    n1 = (2 * width + 4 * (cwidth // 2)) // cols
    (packed1,) = call(
        functools.partial(coarse_weights_kernel, factor), [((cols, n1, cwidth), bf16)]
    )(keep1, send1, flip(send1, "row", 1))

    backs = back_keys(rows, columns)
    flatb = joined(backs)
    rims = len(backs[1])
    bside = len(backs[3])
    middle = count + 2 * rims
    up0, gq0, mid, left_rim, right_rim = call(
        fine_backward_kernel,
        [
            ((count, width), f32),
            ((count, width), bf16),
            ((middle, 2 * width), f32),
            ((bside, 2 * width), bf16),
            ((bside, 2 * width), bf16),
        ],
    )(
        Late(grad_fine.reshape(count, width)),
        grad_merged,
        perm,
        query0,
        kv0,
        chosen(flatb, flat0),
        out_fine,
        Late(jnp.asarray(band_bias(own0, flatb))),
        places(flatb),
        where,
    )
    left_rim, right_rim, packed1 = lax.optimization_barrier((left_rim, right_rim, packed1))
    sums1 = scatter_over_columns(packed1)
    from_right = shifted(left_rim, "col", -1)
    from_left = shifted(right_rim, "col", 1)
    mids = joined(backs[:3])
    own, top_rim, bottom_rim = call(
        fine_fold_kernel,
        [((count, 2 * width), f32), ((rims, 2 * width), bf16), ((rims, 2 * width), bf16)],
        flops=1 << 20,
    )(
        mid,
        from_left,
        from_right,
        chosen(mids, moved(backs[4], 0, -columns)),
        chosen(mids, moved(backs[3], 0, columns)),
    )
    from_below = shifted(top_rim, "row", -1)
    from_above = shifted(bottom_rim, "row", 1)
    from_above, from_below, sums1 = lax.optimization_barrier((from_above, from_below, sums1))
    grad_tokens, gain_part0, keep0, send0 = call(
        fine_last_kernel,
        [
            ((count, width), bf16),
            ((1, width), f32),
            ((count, width), bf16),
            ((count, 5 * width), bf16),
        ],
    )(
        own,
        from_above,
        from_below,
        chosen(own0, moved(backs[2], -rows, 0)),
        chosen(own0, moved(backs[1], rows, 0)),
        gq0,
        up0,
        tok,
        perm,
        normed0,
        att0,
        gain0,
        qkv_fine,
        where,
    )
    n0 = width // cols
    (packed0,) = call(
        functools.partial(fine_weights_kernel, factor), [((cols, n0 + 16, cwidth), bf16)]
    )(keep0, send0, flip(send0, "row", 1), gain_part0, gain_part1)
    sums0 = scatter_over_columns(packed0)

    x, small = reduce_rows(jnp.concatenate([sums1, sums0[:n0]], axis=0), sums0[n0:])
    gains = small.astype(f32) + flip(small, "row", 1).astype(f32)
    x = lax.all_to_all(jnp.broadcast_to(x, (cols,) + x.shape), "col", 0, 0)
    other = flip(x, "row", 1)
    shapes = [
        (2 * cols, 2 * width // cols, cwidth),
        (2 * cols, cwidth // 2 // cols, 3 * cwidth),
        (2 * cols, cwidth // 2 // cols, cwidth),
        (2 * cols, width // 2 // cols, 3 * width),
        (2 * cols, width // 2 // cols, width),
    ]
    vmem = pl.BlockSpec(memory_space=pltpu.VMEM)
    grads = pl.pallas_call(
        unpack_kernel,
        out_shape=[jax.ShapeDtypeStruct(s, bf16) for s in shapes],
        in_specs=[pl.BlockSpec(memory_space=pltpu.SMEM), vmem, vmem],
        out_specs=[pl.BlockSpec(memory_space=pl.ANY)] * len(shapes),
        scratch_shapes=[pltpu.VMEM(s, bf16) for s in shapes]
        + [pltpu.SemaphoreType.DMA((len(shapes),))],
        compiler_params=pltpu.CompilerParams(vmem_limit_bytes=16 << 20),
    )(where, x, other)
    grad_merge, grad_qkv1, grad_out1, grad_qkv0, grad_out0 = (
        g.reshape(-1, g.shape[2]) for g in grads
    )
    return (
        grad_tokens.reshape(rows, columns, width),
        gains[1, :width],
        grad_qkv0,
        grad_out0,
        grad_merge,
        gains[0],
        grad_qkv1,
        grad_out1,
    )


def solution(mesh):
    in_specs = (
        P("row", "col", None),
        P(),
        P(),
        P(),
        P(),
        P(),
        P(),
        P(),
        P("row", "col", None),
        P("row", "col", None),
    )
    out_specs = (P("row", "col", None), P(), P(), P(), P(), P(), P(), P())
    return jax.shard_map(
        per_device, mesh=mesh, in_specs=in_specs, out_specs=out_specs, check_vma=False
    )
```

```python
import functools
import math

import jax
import jax.numpy as jnp
import numpy as np
from jax import lax
from jax.experimental import pallas as pl
from jax.experimental.pallas import tpu as pltpu
from jax.sharding import PartitionSpec as P

HEAD = 64
RADIUS = 3
PAIR = 2 * HEAD
TILE = (8, 16)
VMEM = 32 << 20
NEG = -1e30
norm_eps = 1e-06
f32 = jnp.float32
bf16 = jnp.bfloat16


def shifted(x, axis, by):
    count = lax.axis_size(axis)
    pairs = [(i, i + by) for i in range(count) if 0 <= i + by < count]
    return lax.ppermute(x, axis, pairs)


def flip(x, axis, bit):
    return lax.ppermute(x, axis, [(i, i ^ bit) for i in range(lax.axis_size(axis))])


def add_b(a, b):
    return (a.astype(f32) + b.astype(f32)).astype(bf16)


def grid_piece(rows, columns, length=None):
    piece = [(r, c) for r in rows for c in columns]
    return piece + [None] * ((length or len(piece)) - len(piece))


def merge_order(rows, columns):
    return [
        (2 * a + rp, 2 * b + cp)
        for rp in (0, 1)
        for cp in (0, 1)
        for a in range(rows // 2)
        for b in range(columns // 2)
    ]


def fine_keys(rows, columns):
    near, reach = RADIUS + 1, 2 * RADIUS + 1
    tall = range(-reach, rows + reach)
    side = -(-len(tall) * RADIUS // 16) * 16
    rim = merge_order(near, columns)
    return [
        merge_order(rows, columns),
        [(r - near, c) for r, c in rim],
        [(r + rows, c) for r, c in rim],
        grid_piece(range(-reach, -near), range(columns)),
        grid_piece(range(rows + near, rows + reach), range(columns)),
        grid_piece(tall, range(-RADIUS, 0), side),
        grid_piece(tall, range(columns, columns + RADIUS), side),
    ]


def back_keys(rows, columns):
    tall = range(-RADIUS, rows + RADIUS)
    side = -(-len(tall) * RADIUS // 16) * 16
    return [
        merge_order(rows, columns),
        grid_piece(range(-RADIUS, 0), range(columns)),
        grid_piece(range(rows, rows + RADIUS), range(columns)),
        grid_piece(tall, range(-RADIUS, 0), side),
        grid_piece(tall, range(columns, columns + RADIUS), side),
    ]


def coarse_keys(rows, columns):
    reach = 2 * RADIUS
    tall = range(-reach, rows + reach)
    return [
        grid_piece(range(rows), range(columns)),
        grid_piece(range(-2, 0), range(columns)),
        grid_piece(range(rows, rows + 2), range(columns)),
        grid_piece(range(-reach, -2), range(columns)),
        grid_piece(range(rows + 2, rows + reach), range(columns)),
        grid_piece(tall, range(-reach, 0)),
        grid_piece(tall, range(columns, columns + reach)),
    ]


def coarse_queries(rows, columns):
    reach = RADIUS
    tall = range(-reach, rows + reach)
    side = -(-len(tall) * reach // 16) * 16
    return [
        grid_piece(range(rows), range(columns)),
        grid_piece(range(-reach, 0), range(columns)),
        grid_piece(range(rows, rows + reach), range(columns)),
        grid_piece(tall, range(-reach, 0), side),
        grid_piece(tall, range(columns, columns + reach), side),
    ]


def joined(pieces):
    return [place for piece in pieces for place in piece]


def band_bias(queries, keys):
    bias = np.full((len(queries), len(keys)), NEG, np.float32)
    for i, q in enumerate(queries):
        for j, k in enumerate(keys):
            if q is None:
                inside = j == 0
            else:
                inside = k is not None and max(abs(q[0] - k[0]), abs(q[1] - k[1])) <= RADIUS
            if inside:
                bias[i, j] = 0.0
    return bias


def places(keys):
    return Late(jnp.asarray(np.array([[k[i] if k else 0 for k in keys] for i in (0, 1)], np.int32)))


def one_hot(targets, sources):
    place = {s: j for j, s in enumerate(sources) if s is not None}
    matrix = np.zeros((len(targets), len(sources)), np.float32)
    for i, t in enumerate(targets):
        if t is not None and t in place:
            matrix[i, place[t]] = 1.0
    return matrix.astype(jnp.bfloat16)


def dot(a, b):
    return jnp.dot(a, b, preferred_element_type=f32)


def dot_nt(a, b):
    return lax.dot_general(a, b, (((1,), (1,)), ((), ())), preferred_element_type=f32)


def dot_tn(a, b):
    return lax.dot_general(a, b, (((0,), (0,)), ((), ())), preferred_element_type=f32)


def norm_forward(x, gain):
    values = x.astype(f32)
    scale = lax.rsqrt(jnp.mean(values * values, axis=-1, keepdims=True) + norm_eps)
    return values, scale, (values * scale * gain).astype(bf16)


def norm_backward(values, scale, gain, upstream):
    gain_part = jnp.sum(upstream * values * scale, axis=0, keepdims=True)
    weighted = upstream * gain
    inner = jnp.mean(weighted * values, axis=-1, keepdims=True)
    return weighted * scale - values * (scale * scale * scale) * inner, gain_part


def validity(at, where, rows, columns):
    row = at[0:1, :] + where[0] * rows
    col = at[1:2, :] + where[1] * columns
    ok = (row >= 0) & (row < where[2] * rows) & (col >= 0) & (col < where[3] * columns)
    return jnp.where(ok, 0.0, NEG)


def split_rows(x):
    half = x.shape[1] // 2
    return jnp.concatenate([x[:, :half], x[:, half:]], axis=0)


def join_rows(x):
    half = x.shape[0] // 2
    return jnp.concatenate([x[:half], x[half:]], axis=1)


def head_masks():
    lane = lax.broadcasted_iota(jnp.int32, (1, PAIR), 1)
    return [(lane < HEAD).astype(f32), (lane >= HEAD).astype(f32)]


def masked(x, mask):
    return (x.astype(f32) * mask).astype(bf16)


def probabilities(query, keys, bias):
    weights = jnp.exp(dot_nt(query, keys) * (1.0 / math.sqrt(HEAD)) + bias)
    total = jnp.sum(weights, axis=-1, keepdims=True)
    return weights / jnp.where(total > 0.0, total, 1.0)


def score_gradient(prob, dprob):
    total = jnp.sum(prob * dprob, axis=-1, keepdims=True)
    return (prob * (dprob - total) * (1.0 / math.sqrt(HEAD))).astype(bf16)


def lanes(x, place):
    return x[:, place * PAIR : (place + 1) * PAIR]


def rows_pack_kernel(tok, gc, down_out, up_out):
    rim = down_out.shape[0] - 2 * gc.shape[0]
    both = split_rows(gc[...])
    down_out[:rim] = tok[tok.shape[0] - rim :, :]
    up_out[:rim] = tok[:rim, :]
    down_out[rim:] = both
    up_out[rim:] = both


def columns_pack_kernel(tok, gc, up, down, pick, cpick, right_out, left_out):
    rim = up.shape[0] - 2 * gc.shape[0]
    side = pick.shape[0] // 2
    cside = cpick.shape[0] // 2
    field = jnp.concatenate([tok[...], up[:rim], down[:rim]], axis=0)
    sends = dot(pick[...], field).astype(bf16)
    coarse = jnp.concatenate([gc[...], join_rows(up[rim:]), join_rows(down[rim:])], axis=0)
    csends = dot(cpick[...], coarse).astype(bf16)
    right_out[:side] = sends[:side]
    left_out[:side] = sends[side:]
    right_out[side:] = split_rows(csends[:cside])
    left_out[side:] = split_rows(csends[cside:])


def coarse_pack_kernel(near, up, down, pick, right_out, left_out):
    field = jnp.concatenate([near[...], up[...], down[...]], axis=0)
    sends = dot(pick[...], field).astype(bf16)
    side = right_out.shape[0]
    right_out[...] = sends[:side]
    left_out[...] = sends[side:]


def fine_forward_kernel(
    tok, up, down, left, right, perm, perm_rim, gain, w_qkv, w_out, w_merge, band, at, where,
    merged_out, near_out, down_out, up_out, field_out, proj_out, kv_out, att_out,
):
    width = tok.shape[1]
    count, rim = perm.shape[0], perm_rim.shape[0]
    far = up.shape[0] - 2 * merged_out.shape[0]
    side = (kv_out.shape[0] - count - 2 * far) // 2
    own = dot(perm[...], tok[...]).astype(bf16)
    above = dot(perm_rim[...], up[far - rim : far]).astype(bf16)
    below = dot(perm_rim[...], down[:rim]).astype(bf16)
    inner = jnp.concatenate([own, above, below], axis=0)
    field = jnp.concatenate(
        [inner, up[: far - rim], down[rim:far], left[:side], right[:side]], axis=0
    )
    _, _, normed = norm_forward(field, gain[...])
    field_out[...] = field
    asked = inner.shape[0]
    query = dot(normed[:asked], w_qkv[:, :width]).astype(bf16)
    kv = dot(normed, w_qkv[:, width:]).astype(bf16)
    proj_out[...] = query[:count]
    kv_out[...] = kv
    bias = band[...] + validity(at[...], where, *TILE)
    masks = head_masks()
    parts = []
    for p in range(width // PAIR):
        keys, vals, q = lanes(kv, p), lanes(kv, width // PAIR + p), lanes(query, p)
        total = None
        for mask in masks:
            prob = probabilities(masked(q, mask), keys, bias)
            part = dot(prob.astype(bf16), vals) * mask
            total = part if total is None else total + part
        parts.append(total.astype(bf16))
    attended = jnp.concatenate(parts, axis=1)
    att_out[...] = attended[:count]
    fine = (inner.astype(f32) + dot(attended, w_out[...])).astype(bf16)
    quarter, small = count // 4, rim // 4
    acc = None
    for p in range(4):
        block = fine[p * quarter : (p + 1) * quarter]
        merged_out[:, p * width : (p + 1) * width] = block
        upper = fine[count + p * small : count + (p + 1) * small]
        lower = fine[count + rim + p * small : count + rim + (p + 1) * small]
        block = jnp.concatenate([block, upper, lower], axis=0)
        part = dot(block, w_merge[p * width : (p + 1) * width, :])
        acc = part if acc is None else acc + part
    near = acc.astype(bf16)
    near_out[...] = near
    half = quarter // 2
    down_out[:small] = near[quarter : quarter + small]
    down_out[small:] = near[:half]
    up_out[:half] = near[half:quarter]
    up_out[half:] = near[quarter + small :]


def coarse_upstream_kernel(gc, gup, gdown, gleft, gright, gpick, w_out, up_out, att_out):
    own = gc.shape[0]
    tall, wide = gup.shape[0] - 2 * own, gleft.shape[0] - 2 * (gpick.shape[1] - 3 * own) // 2
    given = [gc[...], join_rows(gup[tall:]), join_rows(gdown[tall:])]
    given += [join_rows(gleft[wide:]), join_rows(gright[wide:])]
    u_b = dot(gpick[...], jnp.concatenate(given, axis=0)).astype(bf16)
    up_out[...] = u_b[:own]
    att_out[...] = dot_nt(u_b, w_out[...]).astype(bf16)


def coarse_kernel(
    near, up, down, left, right, upstream, grad_out, merged, pick, gain, w_qkv, w_merge, band, at, where,
    keep_out, send_out, gain_out, grad_merged_out,
):
    own, width = merged.shape[0], near.shape[1]
    pairs = width // PAIR
    field = jnp.concatenate([near[...], up[...], down[...], left[...], right[...]], axis=0)
    values, scale, normed = norm_forward(field, gain[...])
    kv = dot(normed, w_qkv[:, width:]).astype(bf16)
    picked = dot(pick[...], normed).astype(bf16)
    query = dot(picked, w_qkv[:, :width]).astype(bf16)
    u_b, grad_att = upstream[...], grad_out[...]
    bias = band[...] + validity(at[...], where, TILE[0] // 2, TILE[1] // 2)
    masks = head_masks()
    att, gq, gk, gv = [], [], [], []
    for p in range(pairs):
        keys, vals = lanes(kv, p), lanes(kv, pairs + p)
        q, g = lanes(query, p), lanes(grad_att, p)
        sums = None
        for mask in masks:
            qm, gm = masked(q, mask), masked(g, mask)
            prob = probabilities(qm, keys, bias)
            prob_b = prob.astype(bf16)
            dscore = score_gradient(prob, dot_nt(gm, vals))
            new = (
                dot(prob_b[:own], vals) * mask,
                dot(dscore[:own], keys) * mask,
                dot_tn(dscore[:, :PAIR], qm)[:own],
                dot_tn(prob_b[:, :PAIR], gm)[:own],
            )
            sums = new if sums is None else tuple(a + b for a, b in zip(sums, new))
        for group, part in zip((att, gq, gk, gv), sums):
            group.append(part.astype(bf16))
    attended = jnp.concatenate(att, axis=1)
    grad_proj = jnp.concatenate(gq + gk + gv, axis=1)
    grad_normed = dot_nt(grad_proj, w_qkv[...])
    grad_in, gain_part = norm_backward(values[:own], scale[:own], gain[...], grad_normed)
    gain_out[...] = gain_part
    c_b = (u_b.astype(f32) + grad_in).astype(bf16)
    grad_merged_out[...] = dot_nt(c_b, w_merge[...])
    first = where[0] % 2 == 0
    place = 0
    for x in (merged[...], normed[:own], attended):
        half = x.shape[1] // 2
        low, high = x[:, :half].astype(f32), x[:, half:].astype(f32)
        keep_out[:, place : place + half] = jnp.where(first, low, high).astype(bf16)
        send_out[:, place : place + half] = jnp.where(first, high, low).astype(bf16)
        place += half
    for g in (c_b, grad_proj, u_b):
        send_out[:, place : place + g.shape[1]] = g
        place += g.shape[1]


def weights_kernel(factor, keep, sent, got, fine_keep, fine_got, gain, cgain, out):
    half = keep.shape[1]
    cols = out.shape[2]
    x = jnp.concatenate([keep[...], got[:, :half]], axis=0)
    g = jnp.concatenate([sent[:, half:], got[:, half:]], axis=0)
    wide = half // 2
    narrow = wide // 2
    normed, attended = x[:, wide : wide + narrow], x[:, wide + narrow :]
    parts = [(x[:, :wide], 0)] + [(normed, b) for b in (1, 2, 3)] + [(attended, 4)]
    place = 0
    for a, b in parts:
        part = (dot_tn(a, g[:, b * cols : (b + 1) * cols]) * factor).astype(bf16)
        rows = part.shape[0] // out.shape[0]
        for j in range(out.shape[0]):
            out[j, place : place + rows] = part[j * rows : (j + 1) * rows]
        place += rows
    fine = add_b(fine_keep[...], fine_got[...])
    half = fine.shape[0] // 2
    rows = half // out.shape[0]
    padded = jnp.concatenate([gain[...], jnp.zeros((1, cols - gain.shape[1]), f32)], axis=1)
    gains = jnp.concatenate([cgain[...], padded, jnp.zeros((14, cols), f32)], axis=0)
    gains = (gains * factor).astype(bf16)
    for j in range(out.shape[0]):
        out[j, place : place + rows] = fine[j * rows : (j + 1) * rows]
        out[j, place + rows : place + 2 * rows] = fine[half + j * rows : half + (j + 1) * rows]
        out[j, place + 2 * rows :] = gains


def fine_backward_kernel(
    factor,
    grad_fine, grad_merged, perm, query_in, kv_in, field, att, pick, w_out, w_qkv, gain, band,
    at, where,
    up_out, gq_out, mid_out, left_out, right_out, gain_out, keep_out, send_out,
):
    width = grad_fine.shape[1]
    pairs = width // PAIR
    total = jnp.concatenate([grad_merged[:, p * width : (p + 1) * width] for p in range(4)], axis=0)
    up = dot(perm[...], grad_fine[...]) + total
    up_out[...] = up
    up_b = up.astype(bf16)
    grad_att = dot_nt(up_b, w_out[...]).astype(bf16)
    query = query_in[...]
    kv = dot(pick[...], kv_in[...]).astype(bf16)
    values, scale, normed = norm_forward(dot(pick[...], field[...]), gain[...])
    bias = band[...] + validity(at[...], where, *TILE)
    masks = head_masks()
    middle, side = mid_out.shape[0], left_out.shape[0]
    gq, gk, gv = [], [], []
    for p in range(pairs):
        keys, vals = lanes(kv, p), lanes(kv, pairs + p)
        q, g = lanes(query, p), lanes(grad_att, p)
        sums = None
        for mask in masks:
            qm, gm = masked(q, mask), masked(g, mask)
            prob = probabilities(qm, keys, bias)
            dscore = score_gradient(prob, dot_nt(gm, vals))
            new = (
                dot(dscore, keys) * mask,
                dot_tn(dscore, qm),
                dot_tn(prob.astype(bf16), gm),
            )
            sums = new if sums is None else tuple(a + b for a, b in zip(sums, new))
        gq.append(sums[0].astype(bf16))
        gk.append(sums[1])
        gv.append(sums[2])
    grad_query = jnp.concatenate(gq, axis=1)
    grad_kv = jnp.concatenate(gk + gv, axis=1)
    grad_b = grad_kv.astype(bf16)
    gq_out[...] = grad_query
    mid_out[...] = grad_kv[:middle]
    left_out[...] = grad_b[middle : middle + side]
    right_out[...] = grad_b[middle + side :]
    own = query.shape[0]
    grad_normed = dot_nt(grad_b, w_qkv[:, width:])
    own_normed = dot_nt(grad_query, w_qkv[:, :width])
    ratio = values * scale
    gain_out[...] = jnp.sum(grad_normed * ratio, axis=0, keepdims=True) + jnp.sum(
        own_normed * ratio[:own], axis=0, keepdims=True
    )
    wq = dot_tn(normed[:own], grad_query) * factor
    wkv = dot_tn(normed, grad_b) * factor
    wo = dot_tn(att[...], up_b) * factor
    half = width // 2
    first = where[0] % 2 == 0
    blocks = []
    for rows in (slice(0, half), slice(half, width)):
        high = jnp.concatenate([wq[rows], wkv[rows, :width]], axis=1)
        low = jnp.concatenate([wkv[rows, width:], wo[rows]], axis=1)
        blocks.append(jnp.concatenate([high, low], axis=0))
    keep_out[...] = jnp.where(first, blocks[0], blocks[1]).astype(bf16)
    send_out[...] = jnp.where(first, blocks[1], blocks[0]).astype(bf16)


def fine_fold_kernel(mid, from_left, from_right, place_left, place_right, own_out, top_out, bottom_out):
    folded = mid[...] + dot(place_left[...], from_left[...]) + dot(place_right[...], from_right[...])
    own, rim = own_out.shape[0], top_out.shape[0]
    own_out[...] = folded[:own]
    top_out[...] = folded[own : own + rim].astype(bf16)
    bottom_out[...] = folded[own + rim :].astype(bf16)


def fine_last_kernel(
    own, from_above, from_below, place_above, place_below, gq, up, tok, perm, gain, w_qkv, grad_out
):
    kv = own[...] + dot(place_above[...], from_above[...]) + dot(place_below[...], from_below[...])
    grad_proj = jnp.concatenate([gq[...], kv.astype(bf16)], axis=1)
    values, scale, _ = norm_forward(dot(perm[...], tok[...]), gain[...])
    grad_in, _ = norm_backward(values, scale, gain[...], dot_nt(grad_proj, w_qkv[...]))
    grad_out[...] = dot_tn(perm[...], (up[...] + grad_in).astype(bf16)).astype(bf16)


def unpack_kernel(where, mine, other, merge, qkv1, out1, qkv0, out0, *scratch):
    first = where[0] % 2
    cols, width = mine.shape[0], mine.shape[2]
    half = width // 2
    sems = scratch[-1]
    outs = (merge, qkv1, out1, qkv0, out0)
    m, q1, o1, q0, o0 = scratch[:-1]
    at = 0
    copies = []

    def move(rows, lanes, dst, dst_lanes):
        for src, core in ((mine, first), (other, 1 - first)):
            for j in range(cols):
                dst[core * cols + j, :, dst_lanes] = src[j, rows, lanes]

    def finish(n):
        copies.append(pltpu.make_async_copy(scratch[n], outs[n], sems.at[n]))
        copies[-1].start()

    every = slice(0, width)
    for n in (0, 1, 2):
        rows = outs[n].shape[1]
        for b in range(outs[n].shape[2] // width):
            move(slice(at, at + rows), every, scratch[n], slice(b * width, (b + 1) * width))
            at += rows
        finish(n)
    rows = qkv0.shape[1]
    move(slice(at, at + rows), every, q0, every)
    at += rows
    move(slice(at, at + rows), slice(0, half), q0, slice(width, width + half))
    finish(3)
    move(slice(at, at + rows), slice(half, width), o0, slice(0, half))
    finish(4)
    for copy in copies:
        copy.wait()


class Late:
    def __init__(self, value):
        self.value = value


class Arriving:
    def __init__(self, ref, copy):
        self.ref, self.copy, self.shape = ref, copy, ref.shape

    def __getitem__(self, index):
        if self.copy is not None:
            self.copy.wait()
            self.copy = None
        return self.ref[index]


def call(kernel, outs, flops=1 << 28):
    vmem = pl.BlockSpec(memory_space=pltpu.VMEM)
    smem = pl.BlockSpec(memory_space=pltpu.SMEM)
    anywhere = pl.BlockSpec(memory_space=pl.ANY)

    def run(*args):
        late = [i for i, a in enumerate(args) if isinstance(a, Late)]
        given = [
            pltpu.with_memory_space_constraint(a.value, pltpu.HBM) if isinstance(a, Late) else a
            for a in args
        ]

        def body(*refs):
            ins, results = list(refs[: len(args)]), refs[len(args) : len(args) + len(outs)]
            rest = refs[len(args) + len(outs) :]
            arriving = []
            for n, i in enumerate(late):
                copy = pltpu.make_async_copy(ins[i], rest[n], rest[-1].at[n])
                copy.start()
                ins[i] = Arriving(rest[n], copy)
                arriving.append(ins[i])
            kernel(*ins, *results)
            for operand in arriving:
                if operand.copy is not None:
                    operand.copy.wait()

        scratch = [pltpu.VMEM(given[i].shape, given[i].dtype) for i in late]
        if late:
            scratch.append(pltpu.SemaphoreType.DMA((len(late),)))
        return pl.pallas_call(
            body,
            out_shape=[jax.ShapeDtypeStruct(shape, dtype) for shape, dtype in outs],
            in_specs=[
                anywhere if i in late else smem if a.ndim == 1 else vmem
                for i, a in enumerate(given)
            ],
            out_specs=[vmem] * len(outs),
            scratch_shapes=scratch,
            compiler_params=pltpu.CompilerParams(vmem_limit_bytes=VMEM),
            cost_estimate=pl.CostEstimate(flops=flops, bytes_accessed=4 << 20, transcendentals=0),
        )(*given)

    return run


def scatter_over_columns(x):
    count = lax.axis_size("col")
    pieces = lax.all_to_all(x, "col", 0, 0)
    return jnp.sum(pieces.reshape(count, -1, x.shape[-1]).astype(f32), axis=0).astype(bf16)


def trade_rows(pieces):
    count = lax.axis_size("row") // 2
    groups = [[2 * i + core for i in range(count)] for core in (0, 1)]
    return lax.all_to_all(pieces, "row", 0, 0, axis_index_groups=groups)


def scatter_over_rows(x):
    pieces = trade_rows(x.reshape(lax.axis_size("row") // 2, -1, x.shape[1]))
    return jnp.sum(pieces.astype(f32), axis=0).astype(bf16)


def gather_over_rows(x):
    count = lax.axis_size("row") // 2
    return trade_rows(jnp.broadcast_to(x, (count,) + x.shape)).reshape(-1, x.shape[1])


def per_device(
    tokens,
    gain_fine,
    qkv_fine,
    out_fine,
    w_merge,
    gain_coarse,
    qkv_coarse,
    out_coarse,
    grad_fine,
    grad_coarse,
):
    rows, columns, width = tokens.shape
    crows, ccolumns, cwidth = grad_coarse.shape
    count, ccount = rows * columns, crows * ccolumns
    cols = lax.axis_size("col")
    where = jnp.stack(
        [lax.axis_index("row"), lax.axis_index("col"), lax.axis_size("row"), cols]
    ).astype(jnp.int32)
    factor = 1.0 / math.sqrt(rows * lax.axis_size("row") * columns * cols)
    tok = Late(tokens.reshape(count, width))
    gc = Late(grad_coarse.reshape(ccount, cwidth))
    gain0, gain1 = Late(gain_fine[None, :]), Late(gain_coarse[None, :])
    qkv_fine, out_fine, w_merge = Late(qkv_fine), Late(out_fine), Late(w_merge)
    qkv_coarse, out_coarse = Late(qkv_coarse), Late(out_coarse)

    def moved(piece, dr, dc):
        return [None if p is None else (p[0] + dr, p[1] + dc) for p in piece]

    def chosen(targets, sources):
        return Late(jnp.asarray(one_hot(targets, sources)))

    keys0, keys1 = fine_keys(rows, columns), coarse_keys(crows, ccolumns)
    queries1 = coarse_queries(crows, ccolumns)
    natural = grid_piece(range(rows), range(columns))
    cnatural = queries1[0]
    rim = (2 * RADIUS + 1) * columns
    side, cside = len(keys0[5]), len(queries1[3])
    send_down, send_up = call(
        rows_pack_kernel, [((rim + 2 * ccount, width), bf16)] * 2, flops=1 << 20
    )(tok, gc)
    up = shifted(send_down, "row", 1)
    down = shifted(send_up, "row", -1)
    held = natural + moved(natural[-rim:], -rows, 0) + moved(natural[:rim], rows, 0)
    cheld = cnatural + moved(cnatural, -crows, 0) + moved(cnatural, crows, 0)
    send_right, send_left = call(
        columns_pack_kernel, [((side + 2 * cside, width), bf16)] * 2, flops=1 << 20
    )(
        tok,
        gc,
        up,
        down,
        chosen(moved(keys0[5], 0, columns) + moved(keys0[6], 0, -columns), held),
        chosen(moved(queries1[3], 0, ccolumns) + moved(queries1[4], 0, -ccolumns), cheld),
    )
    left = shifted(send_right, "col", 1)
    right = shifted(send_left, "col", -1)

    flat0 = joined(keys0)
    own0 = keys0[0]
    asked0 = joined(keys0[:3])
    perm = chosen(own0, natural)
    near = len(keys0[1])
    merged, near1, down1, up1, field0, query0, kv0, att0 = call(
        fine_forward_kernel,
        [
            ((ccount, 4 * width), bf16),
            ((ccount + near // 2, cwidth), bf16),
            ((ccount, cwidth), bf16),
            ((ccount, cwidth), bf16),
            ((len(flat0), width), bf16),
            ((count, width), bf16),
            ((len(flat0), 2 * width), bf16),
            ((count, width), bf16),
        ],
    )(
        tok,
        up,
        down,
        left,
        right,
        perm,
        chosen(merge_order(RADIUS + 1, columns), natural[:near]),
        gain0,
        qkv_fine,
        out_fine,
        w_merge,
        Late(jnp.asarray(band_bias(asked0, flat0))),
        places(flat0),
        where,
    )

    above1 = shifted(down1, "row", 1)
    below1 = shifted(up1, "row", -1)
    tall1 = joined(keys1[:5])
    wide1 = len(keys1[5])
    send_right, send_left = call(
        coarse_pack_kernel, [((wide1, cwidth), bf16)] * 2, flops=1 << 20
    )(
        near1,
        above1,
        below1,
        chosen(moved(keys1[5], 0, ccolumns) + moved(keys1[6], 0, -ccolumns), tall1),
    )
    left1 = shifted(send_right, "col", 1)
    right1 = shifted(send_left, "col", -1)

    flat1, ask1 = joined(keys1), joined(queries1)
    upstream1, grad_att1 = call(
        coarse_upstream_kernel,
        [((ccount, cwidth), bf16), ((len(ask1), cwidth), bf16)],
    )(
        gc,
        up,
        down,
        left,
        right,
        chosen(ask1, cheld + queries1[3] + queries1[4]),
        out_coarse,
    )
    kept = (4 * width + 2 * cwidth) // 2
    keep1, send1, gain_part1, grad_merged = call(
        coarse_kernel,
        [
            ((ccount, kept), bf16),
            ((ccount, kept + 5 * cwidth), bf16),
            ((1, cwidth), f32),
            ((ccount, 4 * width), f32),
        ],
    )(
        near1,
        above1,
        below1,
        left1,
        right1,
        upstream1,
        grad_att1,
        merged,
        chosen(ask1, flat1),
        gain1,
        qkv_coarse,
        w_merge,
        Late(jnp.asarray(band_bias(ask1, flat1))),
        places(flat1),
        where,
    )
    got1 = flip(send1, "row", 1)

    backs = back_keys(rows, columns)
    flatb = joined(backs)
    rims = len(backs[1])
    bside = len(backs[3])
    middle = count + 2 * rims
    up0, gq0, mid, left_rim, right_rim, gain_part0, keep0, send0 = call(
        functools.partial(fine_backward_kernel, factor),
        [
            ((count, width), f32),
            ((count, width), bf16),
            ((middle, 2 * width), f32),
            ((bside, 2 * width), bf16),
            ((bside, 2 * width), bf16),
            ((1, width), f32),
            ((width, 2 * width), bf16),
            ((width, 2 * width), bf16),
        ],
    )(
        Late(grad_fine.reshape(count, width)),
        grad_merged,
        perm,
        query0,
        kv0,
        field0,
        att0,
        chosen(flatb, flat0),
        out_fine,
        qkv_fine,
        gain0,
        Late(jnp.asarray(band_bias(own0, flatb))),
        places(flatb),
        where,
    )
    n1 = (2 * width + 4 * (cwidth // 2)) // cols
    n0 = width // cols
    (packed,) = call(
        functools.partial(weights_kernel, factor), [((cols, n1 + n0 + 16, cwidth), bf16)]
    )(keep1, send1, got1, keep0, flip(send0, "row", 1), gain_part0, gain_part1)
    sums = scatter_over_columns(packed)
    from_right = shifted(left_rim, "col", -1)
    from_left = shifted(right_rim, "col", 1)
    sums, from_left, from_right = lax.optimization_barrier((sums, from_left, from_right))
    sums = scatter_over_rows(sums)
    mids = joined(backs[:3])
    own, top_rim, bottom_rim = call(
        fine_fold_kernel,
        [((count, 2 * width), f32), ((rims, 2 * width), bf16), ((rims, 2 * width), bf16)],
        flops=1 << 20,
    )(
        mid,
        from_left,
        from_right,
        chosen(mids, moved(backs[4], 0, -columns)),
        chosen(mids, moved(backs[3], 0, columns)),
    )
    x = gather_over_rows(sums)
    x, top_rim, bottom_rim = lax.optimization_barrier((x, top_rim, bottom_rim))
    from_below = shifted(top_rim, "row", -1)
    from_above = shifted(bottom_rim, "row", 1)
    (grad_tokens,) = call(
        fine_last_kernel,
        [
            ((count, width), bf16),
        ],
    )(
        own,
        from_above,
        from_below,
        chosen(own0, moved(backs[2], -rows, 0)),
        chosen(own0, moved(backs[1], rows, 0)),
        gq0,
        up0,
        tok,
        perm,
        gain0,
        qkv_fine,
    )
    x, small = x[:-16], x[-16:]
    gains = small.astype(f32) + flip(small, "row", 1).astype(f32)
    x = lax.all_to_all(jnp.broadcast_to(x, (cols,) + x.shape), "col", 0, 0)
    x, grad_tokens = lax.optimization_barrier((x, grad_tokens))
    other = flip(x, "row", 1)
    shapes = [
        (2 * cols, 2 * width // cols, cwidth),
        (2 * cols, cwidth // 2 // cols, 3 * cwidth),
        (2 * cols, cwidth // 2 // cols, cwidth),
        (2 * cols, width // 2 // cols, 3 * width),
        (2 * cols, width // 2 // cols, width),
    ]
    vmem = pl.BlockSpec(memory_space=pltpu.VMEM)
    grads = pl.pallas_call(
        unpack_kernel,
        out_shape=[jax.ShapeDtypeStruct(s, bf16) for s in shapes],
        in_specs=[pl.BlockSpec(memory_space=pltpu.SMEM), vmem, vmem],
        out_specs=[pl.BlockSpec(memory_space=pl.ANY)] * len(shapes),
        scratch_shapes=[pltpu.VMEM(s, bf16) for s in shapes]
        + [pltpu.SemaphoreType.DMA((len(shapes),))],
        compiler_params=pltpu.CompilerParams(vmem_limit_bytes=16 << 20),
    )(where, x, other)
    grad_merge, grad_qkv1, grad_out1, grad_qkv0, grad_out0 = (
        g.reshape(-1, g.shape[2]) for g in grads
    )
    return (
        grad_tokens.reshape(rows, columns, width),
        gains[1, :width],
        grad_qkv0,
        grad_out0,
        grad_merge,
        gains[0],
        grad_qkv1,
        grad_out1,
    )


def solution(mesh):
    in_specs = (
        P("row", "col", None),
        P(),
        P(),
        P(),
        P(),
        P(),
        P(),
        P(),
        P("row", "col", None),
        P("row", "col", None),
    )
    out_specs = (P("row", "col", None), P(), P(), P(), P(), P(), P(), P())
    return jax.shard_map(
        per_device, mesh=mesh, in_specs=in_specs, out_specs=out_specs, check_vma=False
    )
```

```python
import functools
import math

import jax
import jax.numpy as jnp
import numpy as np
from jax import lax
from jax.experimental import pallas as pl
from jax.experimental.pallas import tpu as pltpu
from jax.sharding import PartitionSpec as P

HEAD = 64
RADIUS = 3
PAIR = 2 * HEAD
TILE = (8, 16)
VMEM = 20 << 20
NEG = -1e30
norm_eps = 1e-06
f32 = jnp.float32
bf16 = jnp.bfloat16


def shifted(x, axis, by):
    count = lax.axis_size(axis)
    pairs = [(i, i + by) for i in range(count) if 0 <= i + by < count]
    return lax.ppermute(x, axis, pairs)


def flip(x, axis, bit):
    return lax.ppermute(x, axis, [(i, i ^ bit) for i in range(lax.axis_size(axis))])


def add_b(a, b):
    return (a.astype(f32) + b.astype(f32)).astype(bf16)


def grid_piece(rows, columns, length=None):
    piece = [(r, c) for r in rows for c in columns]
    return piece + [None] * ((length or len(piece)) - len(piece))


def merge_order(rows, columns):
    return [
        (2 * a + rp, 2 * b + cp)
        for rp in (0, 1)
        for cp in (0, 1)
        for a in range(rows // 2)
        for b in range(columns // 2)
    ]


def fine_keys(rows, columns):
    near, reach = RADIUS + 1, 2 * RADIUS + 1
    tall = range(-reach, rows + reach)
    side = -(-len(tall) * RADIUS // 16) * 16
    rim = merge_order(near, columns)
    return [
        merge_order(rows, columns),
        [(r - near, c) for r, c in rim],
        [(r + rows, c) for r, c in rim],
        grid_piece(range(-reach, -near), range(columns)),
        grid_piece(range(rows + near, rows + reach), range(columns)),
        grid_piece(tall, range(-RADIUS, 0), side),
        grid_piece(tall, range(columns, columns + RADIUS), side),
    ]


def back_keys(rows, columns):
    tall = range(-RADIUS, rows + RADIUS)
    side = -(-len(tall) * RADIUS // 16) * 16
    return [
        merge_order(rows, columns),
        grid_piece(range(-RADIUS, 0), range(columns)),
        grid_piece(range(rows, rows + RADIUS), range(columns)),
        grid_piece(tall, range(-RADIUS, 0), side),
        grid_piece(tall, range(columns, columns + RADIUS), side),
    ]


def coarse_keys(rows, columns):
    reach = 2 * RADIUS
    tall = range(-reach, rows + reach)
    return [
        grid_piece(range(rows), range(columns)),
        grid_piece(range(-2, 0), range(columns)),
        grid_piece(range(rows, rows + 2), range(columns)),
        grid_piece(range(-reach, -2), range(columns)),
        grid_piece(range(rows + 2, rows + reach), range(columns)),
        grid_piece(tall, range(-reach, 0)),
        grid_piece(tall, range(columns, columns + reach)),
    ]


def coarse_queries(rows, columns):
    reach = RADIUS
    tall = range(-reach, rows + reach)
    side = -(-len(tall) * reach // 16) * 16
    return [
        grid_piece(range(rows), range(columns)),
        grid_piece(range(-reach, 0), range(columns)),
        grid_piece(range(rows, rows + reach), range(columns)),
        grid_piece(tall, range(-reach, 0), side),
        grid_piece(tall, range(columns, columns + reach), side),
    ]


def joined(pieces):
    return [place for piece in pieces for place in piece]


def band_bias(queries, keys):
    bias = np.full((len(queries), len(keys)), NEG, np.float32)
    for i, q in enumerate(queries):
        for j, k in enumerate(keys):
            if q is None:
                inside = j == 0
            else:
                inside = k is not None and max(abs(q[0] - k[0]), abs(q[1] - k[1])) <= RADIUS
            if inside:
                bias[i, j] = 0.0
    return bias


def places(keys):
    return Late(jnp.asarray(np.array([[k[i] if k else 0 for k in keys] for i in (0, 1)], np.int32)))


def one_hot(targets, sources):
    place = {s: j for j, s in enumerate(sources) if s is not None}
    matrix = np.zeros((len(targets), len(sources)), np.float32)
    for i, t in enumerate(targets):
        if t is not None and t in place:
            matrix[i, place[t]] = 1.0
    return matrix.astype(jnp.bfloat16)


def dot(a, b):
    return jnp.dot(a, b, preferred_element_type=f32)


def dot_nt(a, b):
    return lax.dot_general(a, b, (((1,), (1,)), ((), ())), preferred_element_type=f32)


def dot_tn(a, b):
    return lax.dot_general(a, b, (((0,), (0,)), ((), ())), preferred_element_type=f32)


def norm_forward(x, gain):
    values = x.astype(f32)
    scale = lax.rsqrt(jnp.mean(values * values, axis=-1, keepdims=True) + norm_eps)
    return values, scale, (values * scale * gain).astype(bf16)


def norm_backward(values, scale, gain, upstream):
    gain_part = jnp.sum(upstream * values * scale, axis=0, keepdims=True)
    weighted = upstream * gain
    inner = jnp.mean(weighted * values, axis=-1, keepdims=True)
    return weighted * scale - values * (scale * scale * scale) * inner, gain_part


def validity(at, where, rows, columns):
    row = at[0:1, :] + where[0] * rows
    col = at[1:2, :] + where[1] * columns
    ok = (row >= 0) & (row < where[2] * rows) & (col >= 0) & (col < where[3] * columns)
    return jnp.where(ok, 0.0, NEG)


def split_rows(x):
    half = x.shape[1] // 2
    return jnp.concatenate([x[:, :half], x[:, half:]], axis=0)


def join_rows(x):
    half = x.shape[0] // 2
    return jnp.concatenate([x[:half], x[half:]], axis=1)


def head_masks():
    lane = lax.broadcasted_iota(jnp.int32, (1, PAIR), 1)
    return [(lane < HEAD).astype(f32), (lane >= HEAD).astype(f32)]


def masked(x, mask):
    return (x.astype(f32) * mask).astype(bf16)


def probabilities(query, keys, bias):
    weights = jnp.exp(dot_nt(query, keys) * (1.0 / math.sqrt(HEAD)) + bias)
    total = jnp.sum(weights, axis=-1, keepdims=True)
    return weights / jnp.where(total > 0.0, total, 1.0)


def score_gradient(prob, dprob):
    total = jnp.sum(prob * dprob, axis=-1, keepdims=True)
    return (prob * (dprob - total) * (1.0 / math.sqrt(HEAD))).astype(bf16)


def lanes(x, place):
    return x[:, place * PAIR : (place + 1) * PAIR]


def rows_pack_kernel(tok, gc, down_out, up_out):
    rim = down_out.shape[0] - 2 * gc.shape[0]
    both = split_rows(gc[...])
    down_out[:rim] = tok[tok.shape[0] - rim :, :]
    up_out[:rim] = tok[:rim, :]
    down_out[rim:] = both
    up_out[rim:] = both


def columns_pack_kernel(tok, gc, up, down, pick, cpick, right_out, left_out):
    rim = up.shape[0] - 2 * gc.shape[0]
    side = pick.shape[0] // 2
    cside = cpick.shape[0] // 2
    field = jnp.concatenate([tok[...], up[:rim], down[:rim]], axis=0)
    sends = dot(pick[...], field).astype(bf16)
    coarse = jnp.concatenate([gc[...], join_rows(up[rim:]), join_rows(down[rim:])], axis=0)
    csends = dot(cpick[...], coarse).astype(bf16)
    right_out[:side] = sends[:side]
    left_out[:side] = sends[side:]
    right_out[side:] = split_rows(csends[:cside])
    left_out[side:] = split_rows(csends[cside:])


def coarse_pack_kernel(near, up, down, pick, right_out, left_out):
    field = jnp.concatenate([near[...], up[...], down[...]], axis=0)
    sends = dot(pick[...], field).astype(bf16)
    side = right_out.shape[0]
    right_out[...] = sends[:side]
    left_out[...] = sends[side:]


def fine_forward_kernel(
    tok, up, down, left, right, perm, perm_rim, gain, w_qkv, w_out, w_merge, band, at, where,
    merged_out, near_out, down_out, up_out, field_out, proj_out, kv_out, att_out,
):
    width = tok.shape[1]
    count, rim = perm.shape[0], perm_rim.shape[0]
    far = up.shape[0] - 2 * merged_out.shape[0]
    side = (kv_out.shape[0] - count - 2 * far) // 2
    own = dot(perm[...], tok[...]).astype(bf16)
    above = dot(perm_rim[...], up[far - rim : far]).astype(bf16)
    below = dot(perm_rim[...], down[:rim]).astype(bf16)
    inner = jnp.concatenate([own, above, below], axis=0)
    field = jnp.concatenate(
        [inner, up[: far - rim], down[rim:far], left[:side], right[:side]], axis=0
    )
    _, _, normed = norm_forward(field, gain[...])
    field_out[...] = field
    asked = inner.shape[0]
    query = dot(normed[:asked], w_qkv[:, :width]).astype(bf16)
    kv = dot(normed, w_qkv[:, width:]).astype(bf16)
    proj_out[...] = query[:count]
    kv_out[...] = kv
    bias = band[...] + validity(at[...], where, *TILE)
    masks = head_masks()
    parts = []
    for p in range(width // PAIR):
        keys, vals, q = lanes(kv, p), lanes(kv, width // PAIR + p), lanes(query, p)
        total = None
        for mask in masks:
            prob = probabilities(masked(q, mask), keys, bias)
            part = dot(prob.astype(bf16), vals) * mask
            total = part if total is None else total + part
        parts.append(total.astype(bf16))
    attended = jnp.concatenate(parts, axis=1)
    att_out[...] = attended[:count]
    fine = (inner.astype(f32) + dot(attended, w_out[...])).astype(bf16)
    quarter, small = count // 4, rim // 4
    acc = None
    for p in range(4):
        block = fine[p * quarter : (p + 1) * quarter]
        merged_out[:, p * width : (p + 1) * width] = block
        upper = fine[count + p * small : count + (p + 1) * small]
        lower = fine[count + rim + p * small : count + rim + (p + 1) * small]
        block = jnp.concatenate([block, upper, lower], axis=0)
        part = dot(block, w_merge[p * width : (p + 1) * width, :])
        acc = part if acc is None else acc + part
    near = acc.astype(bf16)
    near_out[...] = near
    half = quarter // 2
    down_out[:small] = near[quarter : quarter + small]
    down_out[small:] = near[:half]
    up_out[:half] = near[half:quarter]
    up_out[half:] = near[quarter + small :]


def coarse_upstream_kernel(gc, gup, gdown, gleft, gright, gpick, w_out, up_out, att_out):
    own = gc.shape[0]
    tall, wide = gup.shape[0] - 2 * own, gleft.shape[0] - 2 * (gpick.shape[1] - 3 * own) // 2
    given = [gc[...], join_rows(gup[tall:]), join_rows(gdown[tall:])]
    given += [join_rows(gleft[wide:]), join_rows(gright[wide:])]
    u_b = dot(gpick[...], jnp.concatenate(given, axis=0)).astype(bf16)
    up_out[...] = u_b[:own]
    att_out[...] = dot_nt(u_b, w_out[...]).astype(bf16)


def coarse_kernel(
    near, up, down, left, right, upstream, grad_out, merged, pick, gain, w_qkv, w_merge, band, at, where,
    keep_out, send_out, gain_out, grad_merged_out,
):
    own, width = merged.shape[0], near.shape[1]
    pairs = width // PAIR
    field = jnp.concatenate([near[...], up[...], down[...], left[...], right[...]], axis=0)
    values, scale, normed = norm_forward(field, gain[...])
    kv = dot(normed, w_qkv[:, width:]).astype(bf16)
    picked = dot(pick[...], normed).astype(bf16)
    query = dot(picked, w_qkv[:, :width]).astype(bf16)
    u_b, grad_att = upstream[...], grad_out[...]
    bias = band[...] + validity(at[...], where, TILE[0] // 2, TILE[1] // 2)
    masks = head_masks()
    att, gq, gk, gv = [], [], [], []
    for p in range(pairs):
        keys, vals = lanes(kv, p), lanes(kv, pairs + p)
        q, g = lanes(query, p), lanes(grad_att, p)
        sums = None
        for mask in masks:
            qm, gm = masked(q, mask), masked(g, mask)
            prob = probabilities(qm, keys, bias)
            prob_b = prob.astype(bf16)
            dscore = score_gradient(prob, dot_nt(gm, vals))
            new = (
                dot(prob_b[:own], vals) * mask,
                dot(dscore[:own], keys) * mask,
                dot_tn(dscore[:, :PAIR], qm)[:own],
                dot_tn(prob_b[:, :PAIR], gm)[:own],
            )
            sums = new if sums is None else tuple(a + b for a, b in zip(sums, new))
        for group, part in zip((att, gq, gk, gv), sums):
            group.append(part.astype(bf16))
    attended = jnp.concatenate(att, axis=1)
    grad_proj = jnp.concatenate(gq + gk + gv, axis=1)
    grad_normed = dot_nt(grad_proj, w_qkv[...])
    grad_in, gain_part = norm_backward(values[:own], scale[:own], gain[...], grad_normed)
    gain_out[...] = gain_part
    c_b = (u_b.astype(f32) + grad_in).astype(bf16)
    grad_merged_out[...] = dot_nt(c_b, w_merge[...])
    first = where[0] % 2 == 0
    place = 0
    for x in (merged[...], normed[:own], attended):
        half = x.shape[1] // 2
        low, high = x[:, :half].astype(f32), x[:, half:].astype(f32)
        keep_out[:, place : place + half] = jnp.where(first, low, high).astype(bf16)
        send_out[:, place : place + half] = jnp.where(first, high, low).astype(bf16)
        place += half
    for g in (c_b, grad_proj, u_b):
        send_out[:, place : place + g.shape[1]] = g
        place += g.shape[1]


def weights_kernel(factor, keep, sent, got, fine_keep, fine_got, gain, cgain, out):
    half = keep.shape[1]
    cols = out.shape[2]
    x = jnp.concatenate([keep[...], got[:, :half]], axis=0)
    g = jnp.concatenate([sent[:, half:], got[:, half:]], axis=0)
    wide = half // 2
    narrow = wide // 2
    normed, attended = x[:, wide : wide + narrow], x[:, wide + narrow :]
    parts = [(x[:, :wide], 0)] + [(normed, b) for b in (1, 2, 3)] + [(attended, 4)]
    place = 0
    for a, b in parts:
        part = (dot_tn(a, g[:, b * cols : (b + 1) * cols]) * factor).astype(bf16)
        rows = part.shape[0] // out.shape[0]
        for j in range(out.shape[0]):
            out[j, place : place + rows] = part[j * rows : (j + 1) * rows]
        place += rows
    fine = add_b(fine_keep[...], fine_got[...])
    half = fine.shape[0] // 2
    rows = half // out.shape[0]
    padded = jnp.concatenate([gain[...], jnp.zeros((1, cols - gain.shape[1]), f32)], axis=1)
    gains = jnp.concatenate([cgain[...], padded, jnp.zeros((14, cols), f32)], axis=0)
    gains = (gains * factor).astype(bf16)
    for j in range(out.shape[0]):
        out[j, place : place + rows] = fine[j * rows : (j + 1) * rows]
        out[j, place + rows : place + 2 * rows] = fine[half + j * rows : half + (j + 1) * rows]
        out[j, place + 2 * rows :] = gains


def fine_again_kernel(
    query_in, kv_in, field, pick, gain, band, at, where, kv_out, normed_out, ratio_out, *probs
):
    kv = dot(pick[...], kv_in[...]).astype(bf16)
    values, scale, normed = norm_forward(dot(pick[...], field[...]), gain[...])
    kv_out[...] = kv
    normed_out[...] = normed
    ratio_out[...] = values * scale
    bias = band[...] + validity(at[...], where, *TILE)
    masks = head_masks()
    for h, out in enumerate(probs):
        q = masked(lanes(query_in, h // 2), masks[h % 2])
        out[...] = probabilities(q, lanes(kv, h // 2), bias)


def fine_backward_kernel(
    factor,
    grad_fine, grad_merged, perm, query_in, kv, normed_in, ratio_in, att, p0, p1, p2, p3,
    w_out, w_qkv, gain, where,
    up_out, gq_out, mid_out, left_out, right_out, gain_out, keep_out, send_out,
):
    width = grad_fine.shape[1]
    pairs = width // PAIR
    total = jnp.concatenate([grad_merged[:, p * width : (p + 1) * width] for p in range(4)], axis=0)
    up = dot(perm[...], grad_fine[...]) + total
    up_out[...] = up
    up_b = up.astype(bf16)
    grad_att = dot_nt(up_b, w_out[...]).astype(bf16)
    query = query_in[...]
    normed, ratio = normed_in[...], ratio_in[...]
    masks = head_masks()
    middle, side = mid_out.shape[0], left_out.shape[0]
    gq, gk, gv = [], [], []
    for p in range(pairs):
        keys, vals = lanes(kv, p), lanes(kv, pairs + p)
        q, g = lanes(query, p), lanes(grad_att, p)
        sums = None
        for h, mask in enumerate(masks):
            qm, gm = masked(q, mask), masked(g, mask)
            prob = (p0, p1, p2, p3)[2 * p + h][...]
            dscore = score_gradient(prob, dot_nt(gm, vals))
            new = (
                dot(dscore, keys) * mask,
                dot_tn(dscore, qm),
                dot_tn(prob.astype(bf16), gm),
            )
            sums = new if sums is None else tuple(a + b for a, b in zip(sums, new))
        gq.append(sums[0].astype(bf16))
        gk.append(sums[1])
        gv.append(sums[2])
    grad_query = jnp.concatenate(gq, axis=1)
    grad_kv = jnp.concatenate(gk + gv, axis=1)
    grad_b = grad_kv.astype(bf16)
    gq_out[...] = grad_query
    mid_out[...] = grad_kv[:middle]
    left_out[...] = grad_b[middle : middle + side]
    right_out[...] = grad_b[middle + side :]
    own = query.shape[0]
    grad_normed = dot_nt(grad_b, w_qkv[:, width:])
    own_normed = dot_nt(grad_query, w_qkv[:, :width])
    gain_out[...] = jnp.sum(grad_normed * ratio, axis=0, keepdims=True) + jnp.sum(
        own_normed * ratio[:own], axis=0, keepdims=True
    )
    wq = dot_tn(normed[:own], grad_query) * factor
    wkv = dot_tn(normed, grad_b) * factor
    wo = dot_tn(att[...], up_b) * factor
    half = width // 2
    first = where[0] % 2 == 0
    blocks = []
    for rows in (slice(0, half), slice(half, width)):
        high = jnp.concatenate([wq[rows], wkv[rows, :width]], axis=1)
        low = jnp.concatenate([wkv[rows, width:], wo[rows]], axis=1)
        blocks.append(jnp.concatenate([high, low], axis=0))
    keep_out[...] = jnp.where(first, blocks[0], blocks[1]).astype(bf16)
    send_out[...] = jnp.where(first, blocks[1], blocks[0]).astype(bf16)


def fine_fold_kernel(mid, from_left, from_right, place_left, place_right, own_out, top_out, bottom_out):
    folded = mid[...] + dot(place_left[...], from_left[...]) + dot(place_right[...], from_right[...])
    own, rim = own_out.shape[0], top_out.shape[0]
    own_out[...] = folded[:own]
    top_out[...] = folded[own : own + rim].astype(bf16)
    bottom_out[...] = folded[own + rim :].astype(bf16)


def fine_last_kernel(
    own, from_above, from_below, place_above, place_below, gq, up, tok, perm, gain, w_qkv, grad_out
):
    kv = own[...] + dot(place_above[...], from_above[...]) + dot(place_below[...], from_below[...])
    grad_proj = jnp.concatenate([gq[...], kv.astype(bf16)], axis=1)
    values, scale, _ = norm_forward(dot(perm[...], tok[...]), gain[...])
    grad_in, _ = norm_backward(values, scale, gain[...], dot_nt(grad_proj, w_qkv[...]))
    grad_out[...] = dot_tn(perm[...], (up[...] + grad_in).astype(bf16)).astype(bf16)


def unpack_kernel(where, mine, other, merge, qkv1, out1, qkv0, out0, *scratch):
    first = where[0] % 2
    cols, width = mine.shape[0], mine.shape[2]
    half = width // 2
    sems = scratch[-1]
    outs = (merge, qkv1, out1, qkv0, out0)
    m, q1, o1, q0, o0 = scratch[:-1]
    at = 0
    copies = []

    def move(rows, lanes, dst, dst_lanes):
        for src, core in ((mine, first), (other, 1 - first)):
            for j in range(cols):
                dst[core * cols + j, :, dst_lanes] = src[j, rows, lanes]

    def finish(n):
        copies.append(pltpu.make_async_copy(scratch[n], outs[n], sems.at[n]))
        copies[-1].start()

    every = slice(0, width)
    for n in (0, 1, 2):
        rows = outs[n].shape[1]
        for b in range(outs[n].shape[2] // width):
            move(slice(at, at + rows), every, scratch[n], slice(b * width, (b + 1) * width))
            at += rows
        finish(n)
    rows = qkv0.shape[1]
    move(slice(at, at + rows), every, q0, every)
    at += rows
    move(slice(at, at + rows), slice(0, half), q0, slice(width, width + half))
    finish(3)
    move(slice(at, at + rows), slice(half, width), o0, slice(0, half))
    finish(4)
    for copy in copies:
        copy.wait()


class Late:
    def __init__(self, value):
        self.value = value


class Arriving:
    def __init__(self, ref, copy):
        self.ref, self.copy, self.shape = ref, copy, ref.shape

    def __getitem__(self, index):
        if self.copy is not None:
            self.copy.wait()
            self.copy = None
        return self.ref[index]


def call(kernel, outs, flops=1 << 28):
    vmem = pl.BlockSpec(memory_space=pltpu.VMEM)
    smem = pl.BlockSpec(memory_space=pltpu.SMEM)
    anywhere = pl.BlockSpec(memory_space=pl.ANY)

    def run(*args):
        late = [i for i, a in enumerate(args) if isinstance(a, Late)]
        given = [
            pltpu.with_memory_space_constraint(a.value, pltpu.HBM) if isinstance(a, Late) else a
            for a in args
        ]

        def body(*refs):
            ins, results = list(refs[: len(args)]), refs[len(args) : len(args) + len(outs)]
            rest = refs[len(args) + len(outs) :]
            arriving = []
            for n, i in enumerate(late):
                copy = pltpu.make_async_copy(ins[i], rest[n], rest[-1].at[n])
                copy.start()
                ins[i] = Arriving(rest[n], copy)
                arriving.append(ins[i])
            kernel(*ins, *results)
            for operand in arriving:
                if operand.copy is not None:
                    operand.copy.wait()

        scratch = [pltpu.VMEM(given[i].shape, given[i].dtype) for i in late]
        if late:
            scratch.append(pltpu.SemaphoreType.DMA((len(late),)))
        return pl.pallas_call(
            body,
            out_shape=[jax.ShapeDtypeStruct(shape, dtype) for shape, dtype in outs],
            in_specs=[
                anywhere if i in late else smem if a.ndim == 1 else vmem
                for i, a in enumerate(given)
            ],
            out_specs=[vmem] * len(outs),
            scratch_shapes=scratch,
            compiler_params=pltpu.CompilerParams(vmem_limit_bytes=VMEM),
            cost_estimate=pl.CostEstimate(flops=flops, bytes_accessed=4 << 20, transcendentals=0),
        )(*given)

    return run


def preload(values, after):
    held = [v.value for v in values]
    *held, _ = lax.optimization_barrier((*held, after))
    count = len(held)

    def body(*refs):
        copies = [
            pltpu.make_async_copy(refs[i], refs[count + i], refs[-1].at[i]) for i in range(count)
        ]
        for copy in copies:
            copy.start()
        for copy in copies:
            copy.wait()

    return pl.pallas_call(
        body,
        out_shape=[jax.ShapeDtypeStruct(v.shape, v.dtype) for v in held],
        in_specs=[pl.BlockSpec(memory_space=pl.ANY)] * count,
        out_specs=[pl.BlockSpec(memory_space=pltpu.VMEM)] * count,
        scratch_shapes=[pltpu.SemaphoreType.DMA((count,))],
        compiler_params=pltpu.CompilerParams(vmem_limit_bytes=VMEM),
        cost_estimate=pl.CostEstimate(flops=1 << 20, bytes_accessed=4 << 20, transcendentals=0),
    )(*[pltpu.with_memory_space_constraint(v, pltpu.HBM) for v in held])


def scatter_over_columns(x):
    count = lax.axis_size("col")
    pieces = lax.all_to_all(x, "col", 0, 0)
    return jnp.sum(pieces.reshape(count, -1, x.shape[-1]).astype(f32), axis=0).astype(bf16)


def trade_rows(pieces):
    count = lax.axis_size("row") // 2
    groups = [[2 * i + core for i in range(count)] for core in (0, 1)]
    return lax.all_to_all(pieces, "row", 0, 0, axis_index_groups=groups)


def scatter_over_rows(x):
    pieces = trade_rows(x.reshape(lax.axis_size("row") // 2, -1, x.shape[1]))
    return jnp.sum(pieces.astype(f32), axis=0).astype(bf16)


def gather_over_rows(x):
    count = lax.axis_size("row") // 2
    return trade_rows(jnp.broadcast_to(x, (count,) + x.shape)).reshape(-1, x.shape[1])


def per_device(
    tokens,
    gain_fine,
    qkv_fine,
    out_fine,
    w_merge,
    gain_coarse,
    qkv_coarse,
    out_coarse,
    grad_fine,
    grad_coarse,
):
    rows, columns, width = tokens.shape
    crows, ccolumns, cwidth = grad_coarse.shape
    count, ccount = rows * columns, crows * ccolumns
    cols = lax.axis_size("col")
    where = jnp.stack(
        [lax.axis_index("row"), lax.axis_index("col"), lax.axis_size("row"), cols]
    ).astype(jnp.int32)
    factor = 1.0 / math.sqrt(rows * lax.axis_size("row") * columns * cols)
    tok = Late(tokens.reshape(count, width))
    gc = Late(grad_coarse.reshape(ccount, cwidth))
    gain0, gain1 = Late(gain_fine[None, :]), Late(gain_coarse[None, :])
    qkv_fine, out_fine, w_merge = Late(qkv_fine), Late(out_fine), Late(w_merge)
    qkv_coarse, out_coarse = Late(qkv_coarse), Late(out_coarse)

    def moved(piece, dr, dc):
        return [None if p is None else (p[0] + dr, p[1] + dc) for p in piece]

    def chosen(targets, sources):
        return Late(jnp.asarray(one_hot(targets, sources)))

    keys0, keys1 = fine_keys(rows, columns), coarse_keys(crows, ccolumns)
    queries1 = coarse_queries(crows, ccolumns)
    natural = grid_piece(range(rows), range(columns))
    cnatural = queries1[0]
    rim = (2 * RADIUS + 1) * columns
    side, cside = len(keys0[5]), len(queries1[3])
    send_down, send_up = call(
        rows_pack_kernel, [((rim + 2 * ccount, width), bf16)] * 2, flops=1 << 20
    )(tok, gc)
    up = shifted(send_down, "row", 1)
    down = shifted(send_up, "row", -1)
    held = natural + moved(natural[-rim:], -rows, 0) + moved(natural[:rim], rows, 0)
    cheld = cnatural + moved(cnatural, -crows, 0) + moved(cnatural, crows, 0)
    flat0 = joined(keys0)
    own0 = keys0[0]
    asked0 = joined(keys0[:3])
    near = len(keys0[1])
    perm = chosen(own0, natural)
    tok_v, gc_v, picks, cpicks, *ready0 = preload(
        [
            tok,
            gc,
            chosen(moved(keys0[5], 0, columns) + moved(keys0[6], 0, -columns), held),
            chosen(moved(queries1[3], 0, ccolumns) + moved(queries1[4], 0, -ccolumns), cheld),
            perm,
            chosen(merge_order(RADIUS + 1, columns), natural[:near]),
            gain0,
            qkv_fine,
            out_fine,
            w_merge,
            Late(jnp.asarray(band_bias(asked0, flat0))),
            places(flat0),
        ],
        send_up,
    )
    send_right, send_left = call(
        columns_pack_kernel, [((side + 2 * cside, width), bf16)] * 2, flops=1 << 20
    )(
        tok_v,
        gc_v,
        up,
        down,
        picks,
        cpicks,
    )
    left = shifted(send_right, "col", 1)
    right = shifted(send_left, "col", -1)

    merged, near1, down1, up1, field0, query0, kv0, att0 = call(
        fine_forward_kernel,
        [
            ((ccount, 4 * width), bf16),
            ((ccount + near // 2, cwidth), bf16),
            ((ccount, cwidth), bf16),
            ((ccount, cwidth), bf16),
            ((len(flat0), width), bf16),
            ((count, width), bf16),
            ((len(flat0), 2 * width), bf16),
            ((count, width), bf16),
        ],
    )(
        tok_v,
        up,
        down,
        left,
        right,
        *ready0,
        where,
    )

    above1 = shifted(down1, "row", 1)
    below1 = shifted(up1, "row", -1)
    tall1 = joined(keys1[:5])
    wide1 = len(keys1[5])
    flat1, ask1 = joined(keys1), joined(queries1)
    picks1, pick1, gain_v, qkv_v, merge_v, band1, at1 = preload(
        [
            chosen(moved(keys1[5], 0, ccolumns) + moved(keys1[6], 0, -ccolumns), tall1),
            chosen(ask1, flat1),
            gain1,
            qkv_coarse,
            w_merge,
            Late(jnp.asarray(band_bias(ask1, flat1))),
            places(flat1),
        ],
        near1,
    )
    send_right, send_left = call(
        coarse_pack_kernel, [((wide1, cwidth), bf16)] * 2, flops=1 << 20
    )(
        near1,
        above1,
        below1,
        picks1,
    )
    left1 = shifted(send_right, "col", 1)
    right1 = shifted(send_left, "col", -1)

    flat1, ask1 = joined(keys1), joined(queries1)
    backs = back_keys(rows, columns)
    flatb = joined(backs)
    kvb, normedb, ratiob, *probs = call(
        fine_again_kernel,
        [
            ((len(flatb), 2 * width), bf16),
            ((len(flatb), width), bf16),
            ((len(flatb), width), f32),
        ]
        + [((count, len(flatb)), f32)] * (width // HEAD),
    )(
        query0,
        kv0,
        field0,
        chosen(flatb, flat0),
        gain0,
        Late(jnp.asarray(band_bias(own0, flatb))),
        places(flatb),
        where,
    )
    upstream1, grad_att1 = call(
        coarse_upstream_kernel,
        [((ccount, cwidth), bf16), ((len(ask1), cwidth), bf16)],
    )(
        gc,
        up,
        down,
        left,
        right,
        chosen(ask1, cheld + queries1[3] + queries1[4]),
        out_coarse,
    )
    kept = (4 * width + 2 * cwidth) // 2
    keep1, send1, gain_part1, grad_merged = call(
        coarse_kernel,
        [
            ((ccount, kept), bf16),
            ((ccount, kept + 5 * cwidth), bf16),
            ((1, cwidth), f32),
            ((ccount, 4 * width), f32),
        ],
    )(
        near1,
        above1,
        below1,
        left1,
        right1,
        upstream1,
        grad_att1,
        merged,
        pick1,
        gain_v,
        qkv_v,
        merge_v,
        band1,
        at1,
        where,
    )
    got1 = flip(send1, "row", 1)

    rims = len(backs[1])
    bside = len(backs[3])
    middle = count + 2 * rims
    up0, gq0, mid, left_rim, right_rim, gain_part0, keep0, send0 = call(
        functools.partial(fine_backward_kernel, factor),
        [
            ((count, width), f32),
            ((count, width), bf16),
            ((middle, 2 * width), f32),
            ((bside, 2 * width), bf16),
            ((bside, 2 * width), bf16),
            ((1, width), f32),
            ((width, 2 * width), bf16),
            ((width, 2 * width), bf16),
        ],
    )(
        Late(grad_fine.reshape(count, width)),
        grad_merged,
        perm,
        query0,
        kvb,
        normedb,
        ratiob,
        att0,
        *probs,
        out_fine,
        qkv_fine,
        gain0,
        where,
    )
    n1 = (2 * width + 4 * (cwidth // 2)) // cols
    n0 = width // cols
    (packed,) = call(
        functools.partial(weights_kernel, factor), [((cols, n1 + n0 + 16, cwidth), bf16)]
    )(keep1, send1, got1, keep0, flip(send0, "row", 1), gain_part0, gain_part1)
    sums = scatter_over_columns(packed)
    from_right = shifted(left_rim, "col", -1)
    from_left = shifted(right_rim, "col", 1)
    sums, from_left, from_right = lax.optimization_barrier((sums, from_left, from_right))
    sums = scatter_over_rows(sums)
    mids = joined(backs[:3])
    own, top_rim, bottom_rim = call(
        fine_fold_kernel,
        [((count, 2 * width), f32), ((rims, 2 * width), bf16), ((rims, 2 * width), bf16)],
        flops=1 << 20,
    )(
        mid,
        from_left,
        from_right,
        chosen(mids, moved(backs[4], 0, -columns)),
        chosen(mids, moved(backs[3], 0, columns)),
    )
    x = gather_over_rows(sums)
    x, top_rim, bottom_rim = lax.optimization_barrier((x, top_rim, bottom_rim))
    from_below = shifted(top_rim, "row", -1)
    from_above = shifted(bottom_rim, "row", 1)
    (grad_tokens,) = call(
        fine_last_kernel,
        [
            ((count, width), bf16),
        ],
    )(
        own,
        from_above,
        from_below,
        chosen(own0, moved(backs[2], -rows, 0)),
        chosen(own0, moved(backs[1], rows, 0)),
        gq0,
        up0,
        tok,
        perm,
        gain0,
        qkv_fine,
    )
    x, small = x[:-16], x[-16:]
    x = lax.all_to_all(jnp.broadcast_to(x, (cols,) + x.shape), "col", 0, 0)
    gains = small.astype(f32) + flip(small, "row", 1).astype(f32)
    gain_sums = (gains[1, :width], gains[0])
    x, grad_tokens, gain_sums = lax.optimization_barrier((x, grad_tokens, gain_sums))
    other = flip(x, "row", 1)
    shapes = [
        (2 * cols, 2 * width // cols, cwidth),
        (2 * cols, cwidth // 2 // cols, 3 * cwidth),
        (2 * cols, cwidth // 2 // cols, cwidth),
        (2 * cols, width // 2 // cols, 3 * width),
        (2 * cols, width // 2 // cols, width),
    ]
    vmem = pl.BlockSpec(memory_space=pltpu.VMEM)
    grads = pl.pallas_call(
        unpack_kernel,
        out_shape=[jax.ShapeDtypeStruct(s, bf16) for s in shapes],
        in_specs=[pl.BlockSpec(memory_space=pltpu.SMEM), vmem, vmem],
        out_specs=[pl.BlockSpec(memory_space=pl.ANY)] * len(shapes),
        scratch_shapes=[pltpu.VMEM(s, bf16) for s in shapes]
        + [pltpu.SemaphoreType.DMA((len(shapes),))],
        compiler_params=pltpu.CompilerParams(vmem_limit_bytes=16 << 20),
    )(where, x, other)
    grad_merge, grad_qkv1, grad_out1, grad_qkv0, grad_out0 = (
        g.reshape(-1, g.shape[2]) for g in grads
    )
    return (
        grad_tokens.reshape(rows, columns, width),
        gain_sums[0],
        grad_qkv0,
        grad_out0,
        grad_merge,
        gain_sums[1],
        grad_qkv1,
        grad_out1,
    )


def solution(mesh):
    in_specs = (
        P("row", "col", None),
        P(),
        P(),
        P(),
        P(),
        P(),
        P(),
        P(),
        P("row", "col", None),
        P("row", "col", None),
    )
    out_specs = (P("row", "col", None), P(), P(), P(), P(), P(), P(), P())
    return jax.shard_map(
        per_device, mesh=mesh, in_specs=in_specs, out_specs=out_specs, check_vma=False
    )
```

```python
import functools
import math

import jax
import jax.numpy as jnp
import numpy as np
from jax import lax
from jax.experimental import pallas as pl
from jax.experimental.pallas import tpu as pltpu
from jax.sharding import PartitionSpec as P

HEAD = 64
RADIUS = 3
PAIR = 2 * HEAD
TILE = (8, 16)
VMEM = 20 << 20
NEG = -1e30
norm_eps = 1e-06
f32 = jnp.float32
bf16 = jnp.bfloat16


def shifted(x, axis, by):
    count = lax.axis_size(axis)
    pairs = [(i, i + by) for i in range(count) if 0 <= i + by < count]
    return lax.ppermute(x, axis, pairs)


def flip(x, axis, bit):
    return lax.ppermute(x, axis, [(i, i ^ bit) for i in range(lax.axis_size(axis))])


def add_b(a, b):
    return (a.astype(f32) + b.astype(f32)).astype(bf16)


def grid_piece(rows, columns, length=None):
    piece = [(r, c) for r in rows for c in columns]
    return piece + [None] * ((length or len(piece)) - len(piece))


def merge_order(rows, columns):
    return [
        (2 * a + rp, 2 * b + cp)
        for rp in (0, 1)
        for cp in (0, 1)
        for a in range(rows // 2)
        for b in range(columns // 2)
    ]


def fine_keys(rows, columns):
    near, reach = RADIUS + 1, 2 * RADIUS + 1
    tall = range(-reach, rows + reach)
    side = -(-len(tall) * RADIUS // 16) * 16
    rim = merge_order(near, columns)
    return [
        merge_order(rows, columns),
        [(r - near, c) for r, c in rim],
        [(r + rows, c) for r, c in rim],
        grid_piece(range(-reach, -near), range(columns)),
        grid_piece(range(rows + near, rows + reach), range(columns)),
        grid_piece(tall, range(-RADIUS, 0), side),
        grid_piece(tall, range(columns, columns + RADIUS), side),
    ]


def back_keys(rows, columns):
    tall = range(-RADIUS, rows + RADIUS)
    side = -(-len(tall) * RADIUS // 16) * 16
    return [
        merge_order(rows, columns),
        grid_piece(range(-RADIUS, 0), range(columns)),
        grid_piece(range(rows, rows + RADIUS), range(columns)),
        grid_piece(tall, range(-RADIUS, 0), side),
        grid_piece(tall, range(columns, columns + RADIUS), side),
    ]


def coarse_keys(rows, columns):
    reach = 2 * RADIUS
    tall = range(-reach, rows + reach)
    return [
        grid_piece(range(rows), range(columns)),
        grid_piece(range(-2, 0), range(columns)),
        grid_piece(range(rows, rows + 2), range(columns)),
        grid_piece(range(-reach, -2), range(columns)),
        grid_piece(range(rows + 2, rows + reach), range(columns)),
        grid_piece(tall, range(-reach, 0)),
        grid_piece(tall, range(columns, columns + reach)),
    ]


def coarse_queries(rows, columns):
    reach = RADIUS
    tall = range(-reach, rows + reach)
    side = -(-len(tall) * reach // 16) * 16
    return [
        grid_piece(range(rows), range(columns)),
        grid_piece(range(-reach, 0), range(columns)),
        grid_piece(range(rows, rows + reach), range(columns)),
        grid_piece(tall, range(-reach, 0), side),
        grid_piece(tall, range(columns, columns + reach), side),
    ]


def joined(pieces):
    return [place for piece in pieces for place in piece]


def band_bias(queries, keys):
    bias = np.full((len(queries), len(keys)), NEG, np.float32)
    for i, q in enumerate(queries):
        for j, k in enumerate(keys):
            if q is None:
                inside = j == 0
            else:
                inside = k is not None and max(abs(q[0] - k[0]), abs(q[1] - k[1])) <= RADIUS
            if inside:
                bias[i, j] = 0.0
    return bias


def places(keys):
    return Late(jnp.asarray(np.array([[k[i] if k else 0 for k in keys] for i in (0, 1)], np.int32)))


def one_hot(targets, sources):
    place = {s: j for j, s in enumerate(sources) if s is not None}
    matrix = np.zeros((len(targets), len(sources)), np.float32)
    for i, t in enumerate(targets):
        if t is not None and t in place:
            matrix[i, place[t]] = 1.0
    return matrix.astype(jnp.bfloat16)


def dot(a, b):
    return jnp.dot(a, b, preferred_element_type=f32)


def dot_nt(a, b):
    return lax.dot_general(a, b, (((1,), (1,)), ((), ())), preferred_element_type=f32)


def dot_tn(a, b):
    return lax.dot_general(a, b, (((0,), (0,)), ((), ())), preferred_element_type=f32)


def norm_forward(x, gain):
    values = x.astype(f32)
    scale = lax.rsqrt(jnp.mean(values * values, axis=-1, keepdims=True) + norm_eps)
    return values, scale, (values * scale * gain).astype(bf16)


def norm_backward(values, scale, gain, upstream):
    gain_part = jnp.sum(upstream * values * scale, axis=0, keepdims=True)
    weighted = upstream * gain
    inner = jnp.mean(weighted * values, axis=-1, keepdims=True)
    return weighted * scale - values * (scale * scale * scale) * inner, gain_part


def validity(at, where, rows, columns):
    row = at[0:1, :] + where[0] * rows
    col = at[1:2, :] + where[1] * columns
    ok = (row >= 0) & (row < where[2] * rows) & (col >= 0) & (col < where[3] * columns)
    return jnp.where(ok, 0.0, NEG)


def split_rows(x):
    half = x.shape[1] // 2
    return jnp.concatenate([x[:, :half], x[:, half:]], axis=0)


def join_rows(x):
    half = x.shape[0] // 2
    return jnp.concatenate([x[:half], x[half:]], axis=1)


def head_masks():
    lane = lax.broadcasted_iota(jnp.int32, (1, PAIR), 1)
    return [(lane < HEAD).astype(f32), (lane >= HEAD).astype(f32)]


def masked(x, mask):
    return (x.astype(f32) * mask).astype(bf16)


def probabilities(query, keys, bias):
    weights = jnp.exp(dot_nt(query, keys) * (1.0 / math.sqrt(HEAD)) + bias)
    total = jnp.sum(weights, axis=-1, keepdims=True)
    return weights / jnp.where(total > 0.0, total, 1.0)


def score_gradient(prob, dprob):
    total = jnp.sum(prob * dprob, axis=-1, keepdims=True)
    return (prob * (dprob - total) * (1.0 / math.sqrt(HEAD))).astype(bf16)


def lanes(x, place):
    return x[:, place * PAIR : (place + 1) * PAIR]


def rows_pack_kernel(tok, gc, down_out, up_out):
    rim = down_out.shape[0] - 2 * gc.shape[0]
    both = split_rows(gc[...])
    down_out[:rim] = tok[tok.shape[0] - rim :, :]
    up_out[:rim] = tok[:rim, :]
    down_out[rim:] = both
    up_out[rim:] = both


def columns_pack_kernel(tok, gc, up, down, pick, cpick, right_out, left_out):
    rim = up.shape[0] - 2 * gc.shape[0]
    side = pick.shape[0] // 2
    cside = cpick.shape[0] // 2
    field = jnp.concatenate([tok[...], up[:rim], down[:rim]], axis=0)
    sends = dot(pick[...], field).astype(bf16)
    coarse = jnp.concatenate([gc[...], join_rows(up[rim:]), join_rows(down[rim:])], axis=0)
    csends = dot(cpick[...], coarse).astype(bf16)
    right_out[:side] = sends[:side]
    left_out[:side] = sends[side:]
    right_out[side:] = split_rows(csends[:cside])
    left_out[side:] = split_rows(csends[cside:])


def coarse_pack_kernel(near, up, down, pick, right_out, left_out):
    field = jnp.concatenate([near[...], up[...], down[...]], axis=0)
    sends = dot(pick[...], field).astype(bf16)
    side = right_out.shape[0]
    right_out[...] = sends[:side]
    left_out[...] = sends[side:]


def fine_forward_kernel(
    tok, up, down, left, right, perm, perm_rim, gain, w_qkv, w_out, w_merge, band, at, where,
    merged_out, near_out, down_out, up_out, field_out, proj_out, kv_out, att_out,
):
    width = tok.shape[1]
    count, rim = perm.shape[0], perm_rim.shape[0]
    far = up.shape[0] - 2 * merged_out.shape[0]
    side = (kv_out.shape[0] - count - 2 * far) // 2
    own = dot(perm[...], tok[...]).astype(bf16)
    above = dot(perm_rim[...], up[far - rim : far]).astype(bf16)
    below = dot(perm_rim[...], down[:rim]).astype(bf16)
    inner = jnp.concatenate([own, above, below], axis=0)
    field = jnp.concatenate(
        [inner, up[: far - rim], down[rim:far], left[:side], right[:side]], axis=0
    )
    _, _, normed = norm_forward(field, gain[...])
    field_out[...] = field
    asked = inner.shape[0]
    query = dot(normed[:asked], w_qkv[:, :width]).astype(bf16)
    kv = dot(normed, w_qkv[:, width:]).astype(bf16)
    proj_out[...] = query[:count]
    kv_out[...] = kv
    bias = band[...] + validity(at[...], where, *TILE)
    masks = head_masks()
    parts = []
    for p in range(width // PAIR):
        keys, vals, q = lanes(kv, p), lanes(kv, width // PAIR + p), lanes(query, p)
        total = None
        for mask in masks:
            prob = probabilities(masked(q, mask), keys, bias)
            part = dot(prob.astype(bf16), vals) * mask
            total = part if total is None else total + part
        parts.append(total.astype(bf16))
    attended = jnp.concatenate(parts, axis=1)
    att_out[...] = attended[:count]
    fine = (inner.astype(f32) + dot(attended, w_out[...])).astype(bf16)
    quarter, small = count // 4, rim // 4
    acc = None
    for p in range(4):
        block = fine[p * quarter : (p + 1) * quarter]
        merged_out[:, p * width : (p + 1) * width] = block
        upper = fine[count + p * small : count + (p + 1) * small]
        lower = fine[count + rim + p * small : count + rim + (p + 1) * small]
        block = jnp.concatenate([block, upper, lower], axis=0)
        part = dot(block, w_merge[p * width : (p + 1) * width, :])
        acc = part if acc is None else acc + part
    near = acc.astype(bf16)
    near_out[...] = near
    half = quarter // 2
    down_out[:small] = near[quarter : quarter + small]
    down_out[small:] = near[:half]
    up_out[:half] = near[half:quarter]
    up_out[half:] = near[quarter + small :]


def coarse_upstream_kernel(gc, gup, gdown, gleft, gright, gpick, w_out, up_out, att_out):
    own = gc.shape[0]
    tall, wide = gup.shape[0] - 2 * own, gleft.shape[0] - 2 * (gpick.shape[1] - 3 * own) // 2
    given = [gc[...], join_rows(gup[tall:]), join_rows(gdown[tall:])]
    given += [join_rows(gleft[wide:]), join_rows(gright[wide:])]
    u_b = dot(gpick[...], jnp.concatenate(given, axis=0)).astype(bf16)
    up_out[...] = u_b[:own]
    att_out[...] = dot_nt(u_b, w_out[...]).astype(bf16)


def coarse_kernel(
    near, up, down, left, right, upstream, grad_out, merged, pick, gain, w_qkv, w_merge, band, at, where,
    keep_out, send_out, gain_out, grad_merged_out,
):
    own, width = merged.shape[0], near.shape[1]
    pairs = width // PAIR
    field = jnp.concatenate([near[...], up[...], down[...], left[...], right[...]], axis=0)
    values, scale, normed = norm_forward(field, gain[...])
    kv = dot(normed, w_qkv[:, width:]).astype(bf16)
    picked = dot(pick[...], normed).astype(bf16)
    query = dot(picked, w_qkv[:, :width]).astype(bf16)
    u_b, grad_att = upstream[...], grad_out[...]
    bias = band[...] + validity(at[...], where, TILE[0] // 2, TILE[1] // 2)
    masks = head_masks()
    att, gq, gk, gv = [], [], [], []
    for p in range(pairs):
        keys, vals = lanes(kv, p), lanes(kv, pairs + p)
        q, g = lanes(query, p), lanes(grad_att, p)
        sums = None
        for mask in masks:
            qm, gm = masked(q, mask), masked(g, mask)
            prob = probabilities(qm, keys, bias)
            prob_b = prob.astype(bf16)
            dscore = score_gradient(prob, dot_nt(gm, vals))
            new = (
                dot(prob_b[:own], vals) * mask,
                dot(dscore[:own], keys) * mask,
                dot_tn(dscore[:, :PAIR], qm)[:own],
                dot_tn(prob_b[:, :PAIR], gm)[:own],
            )
            sums = new if sums is None else tuple(a + b for a, b in zip(sums, new))
        for group, part in zip((att, gq, gk, gv), sums):
            group.append(part.astype(bf16))
    attended = jnp.concatenate(att, axis=1)
    grad_proj = jnp.concatenate(gq + gk + gv, axis=1)
    grad_normed = dot_nt(grad_proj, w_qkv[...])
    grad_in, gain_part = norm_backward(values[:own], scale[:own], gain[...], grad_normed)
    gain_out[...] = gain_part
    c_b = (u_b.astype(f32) + grad_in).astype(bf16)
    grad_merged_out[...] = dot_nt(c_b, w_merge[...])
    first = where[0] % 2 == 0
    place = 0
    for x in (merged[...], normed[:own], attended):
        half = x.shape[1] // 2
        low, high = x[:, :half].astype(f32), x[:, half:].astype(f32)
        keep_out[:, place : place + half] = jnp.where(first, low, high).astype(bf16)
        send_out[:, place : place + half] = jnp.where(first, high, low).astype(bf16)
        place += half
    for g in (c_b, grad_proj, u_b):
        send_out[:, place : place + g.shape[1]] = g
        place += g.shape[1]


def weights_kernel(factor, keep, sent, got, fine_keep, fine_got, gain, cgain, out):
    half = keep.shape[1]
    cols = out.shape[2]
    x = jnp.concatenate([keep[...], got[:, :half]], axis=0)
    g = jnp.concatenate([sent[:, half:], got[:, half:]], axis=0)
    wide = half // 2
    narrow = wide // 2
    normed, attended = x[:, wide : wide + narrow], x[:, wide + narrow :]
    parts = [(x[:, :wide], 0)] + [(normed, b) for b in (1, 2, 3)] + [(attended, 4)]
    place = 0
    for a, b in parts:
        part = (dot_tn(a, g[:, b * cols : (b + 1) * cols]) * factor).astype(bf16)
        rows = part.shape[0] // out.shape[0]
        for j in range(out.shape[0]):
            out[j, place : place + rows] = part[j * rows : (j + 1) * rows]
        place += rows
    fine = add_b(fine_keep[...], fine_got[...])
    half = fine.shape[0] // 2
    rows = half // out.shape[0]
    padded = jnp.concatenate([gain[...], jnp.zeros((1, cols - gain.shape[1]), f32)], axis=1)
    gains = jnp.concatenate([cgain[...], padded, jnp.zeros((14, cols), f32)], axis=0)
    gains = (gains * factor).astype(bf16)
    for j in range(out.shape[0]):
        out[j, place : place + rows] = fine[j * rows : (j + 1) * rows]
        out[j, place + rows : place + 2 * rows] = fine[half + j * rows : half + (j + 1) * rows]
        out[j, place + 2 * rows :] = gains


def fine_again_kernel(
    query_in, kv_in, field, pick, gain, band, at, where, kv_out, normed_out, ratio_out, *probs
):
    kv = dot(pick[...], kv_in[...]).astype(bf16)
    values, scale, normed = norm_forward(dot(pick[...], field[...]), gain[...])
    kv_out[...] = kv
    normed_out[...] = normed
    ratio_out[...] = values * scale
    bias = band[...] + validity(at[...], where, *TILE)
    masks = head_masks()
    for h, out in enumerate(probs):
        q = masked(lanes(query_in, h // 2), masks[h % 2])
        out[...] = probabilities(q, lanes(kv, h // 2), bias)


def fine_backward_kernel(
    factor,
    grad_fine, grad_merged, perm, query_in, kv, normed_in, ratio_in, att, p0, p1, p2, p3,
    w_out, w_qkv, gain, where,
    up_out, gq_out, mid_out, left_out, right_out, gain_out, keep_out, send_out,
):
    width = grad_fine.shape[1]
    pairs = width // PAIR
    total = jnp.concatenate([grad_merged[:, p * width : (p + 1) * width] for p in range(4)], axis=0)
    up = dot(perm[...], grad_fine[...]) + total
    up_out[...] = up
    up_b = up.astype(bf16)
    grad_att = dot_nt(up_b, w_out[...]).astype(bf16)
    query = query_in[...]
    normed, ratio = normed_in[...], ratio_in[...]
    masks = head_masks()
    middle, side = mid_out.shape[0], left_out.shape[0]
    gq, gk, gv = [], [], []
    for p in range(pairs):
        keys, vals = lanes(kv, p), lanes(kv, pairs + p)
        q, g = lanes(query, p), lanes(grad_att, p)
        sums = None
        for h, mask in enumerate(masks):
            qm, gm = masked(q, mask), masked(g, mask)
            prob = (p0, p1, p2, p3)[2 * p + h][...]
            dscore = score_gradient(prob, dot_nt(gm, vals))
            new = (
                dot(dscore, keys) * mask,
                dot_tn(dscore, qm),
                dot_tn(prob.astype(bf16), gm),
            )
            sums = new if sums is None else tuple(a + b for a, b in zip(sums, new))
        gq.append(sums[0].astype(bf16))
        gk.append(sums[1])
        gv.append(sums[2])
    grad_query = jnp.concatenate(gq, axis=1)
    grad_kv = jnp.concatenate(gk + gv, axis=1)
    grad_b = grad_kv.astype(bf16)
    gq_out[...] = grad_query
    mid_out[...] = grad_kv[:middle]
    left_out[...] = grad_b[middle : middle + side]
    right_out[...] = grad_b[middle + side :]
    own = query.shape[0]
    grad_normed = dot_nt(grad_b, w_qkv[:, width:])
    own_normed = dot_nt(grad_query, w_qkv[:, :width])
    gain_out[...] = jnp.sum(grad_normed * ratio, axis=0, keepdims=True) + jnp.sum(
        own_normed * ratio[:own], axis=0, keepdims=True
    )
    wq = dot_tn(normed[:own], grad_query) * factor
    wkv = dot_tn(normed, grad_b) * factor
    wo = dot_tn(att[...], up_b) * factor
    half = width // 2
    first = where[0] % 2 == 0
    blocks = []
    for rows in (slice(0, half), slice(half, width)):
        high = jnp.concatenate([wq[rows], wkv[rows, :width]], axis=1)
        low = jnp.concatenate([wkv[rows, width:], wo[rows]], axis=1)
        blocks.append(jnp.concatenate([high, low], axis=0))
    keep_out[...] = jnp.where(first, blocks[0], blocks[1]).astype(bf16)
    send_out[...] = jnp.where(first, blocks[1], blocks[0]).astype(bf16)


def fine_fold_kernel(mid, from_left, from_right, place_left, place_right, own_out, top_out, bottom_out):
    folded = mid[...] + dot(place_left[...], from_left[...]) + dot(place_right[...], from_right[...])
    own, rim = own_out.shape[0], top_out.shape[0]
    own_out[...] = folded[:own]
    top_out[...] = folded[own : own + rim].astype(bf16)
    bottom_out[...] = folded[own + rim :].astype(bf16)


def fine_last_kernel(
    own, from_above, from_below, place_above, place_below, gq, up, tok, perm, gain, w_qkv, grad_out
):
    kv = own[...] + dot(place_above[...], from_above[...]) + dot(place_below[...], from_below[...])
    grad_proj = jnp.concatenate([gq[...], kv.astype(bf16)], axis=1)
    values, scale, _ = norm_forward(dot(perm[...], tok[...]), gain[...])
    grad_in, _ = norm_backward(values, scale, gain[...], dot_nt(grad_proj, w_qkv[...]))
    grad_out[...] = dot_tn(perm[...], (up[...] + grad_in).astype(bf16)).astype(bf16)


def unpack_kernel(where, mine, other, merge, qkv1, out1, qkv0, out0, *scratch):
    first = where[0] % 2
    cols, width = mine.shape[0], mine.shape[2]
    half = width // 2
    sems = scratch[-1]
    outs = (merge, qkv1, out1, qkv0, out0)
    m, q1, o1, q0, o0 = scratch[:-1]
    at = 0
    copies = []

    def move(rows, lanes, dst, dst_lanes):
        for src, core in ((mine, first), (other, 1 - first)):
            for j in range(cols):
                dst[core * cols + j, :, dst_lanes] = src[j, rows, lanes]

    def finish(n):
        copies.append(pltpu.make_async_copy(scratch[n], outs[n], sems.at[n]))
        copies[-1].start()

    every = slice(0, width)
    for n in (0, 1, 2):
        rows = outs[n].shape[1]
        for b in range(outs[n].shape[2] // width):
            move(slice(at, at + rows), every, scratch[n], slice(b * width, (b + 1) * width))
            at += rows
        finish(n)
    rows = qkv0.shape[1]
    move(slice(at, at + rows), every, q0, every)
    at += rows
    move(slice(at, at + rows), slice(0, half), q0, slice(width, width + half))
    finish(3)
    move(slice(at, at + rows), slice(half, width), o0, slice(0, half))
    finish(4)
    for copy in copies:
        copy.wait()


class Late:
    def __init__(self, value):
        self.value = value


class Arriving:
    def __init__(self, ref, copy):
        self.ref, self.copy, self.shape = ref, copy, ref.shape

    def __getitem__(self, index):
        if self.copy is not None:
            self.copy.wait()
            self.copy = None
        return self.ref[index]


def call(kernel, outs, flops=1 << 28):
    vmem = pl.BlockSpec(memory_space=pltpu.VMEM)
    smem = pl.BlockSpec(memory_space=pltpu.SMEM)
    anywhere = pl.BlockSpec(memory_space=pl.ANY)

    def run(*args):
        late = [i for i, a in enumerate(args) if isinstance(a, Late)]
        given = [
            pltpu.with_memory_space_constraint(a.value, pltpu.HBM) if isinstance(a, Late) else a
            for a in args
        ]

        def body(*refs):
            ins, results = list(refs[: len(args)]), refs[len(args) : len(args) + len(outs)]
            rest = refs[len(args) + len(outs) :]
            arriving = []
            for n, i in enumerate(late):
                copy = pltpu.make_async_copy(ins[i], rest[n], rest[-1].at[n])
                copy.start()
                ins[i] = Arriving(rest[n], copy)
                arriving.append(ins[i])
            kernel(*ins, *results)
            for operand in arriving:
                if operand.copy is not None:
                    operand.copy.wait()

        scratch = [pltpu.VMEM(given[i].shape, given[i].dtype) for i in late]
        if late:
            scratch.append(pltpu.SemaphoreType.DMA((len(late),)))
        return pl.pallas_call(
            body,
            out_shape=[jax.ShapeDtypeStruct(shape, dtype) for shape, dtype in outs],
            in_specs=[
                anywhere if i in late else smem if a.ndim == 1 else vmem
                for i, a in enumerate(given)
            ],
            out_specs=[vmem] * len(outs),
            scratch_shapes=scratch,
            compiler_params=pltpu.CompilerParams(vmem_limit_bytes=VMEM),
            cost_estimate=pl.CostEstimate(flops=flops, bytes_accessed=4 << 20, transcendentals=0),
        )(*given)

    return run


def preload(values, after):
    held = [v.value for v in values]
    *held, _ = lax.optimization_barrier((*held, after))
    count = len(held)

    def body(*refs):
        copies = [
            pltpu.make_async_copy(refs[i], refs[count + i], refs[-1].at[i]) for i in range(count)
        ]
        for copy in copies:
            copy.start()
        for copy in copies:
            copy.wait()

    return pl.pallas_call(
        body,
        out_shape=[jax.ShapeDtypeStruct(v.shape, v.dtype) for v in held],
        in_specs=[pl.BlockSpec(memory_space=pl.ANY)] * count,
        out_specs=[pl.BlockSpec(memory_space=pltpu.VMEM)] * count,
        scratch_shapes=[pltpu.SemaphoreType.DMA((count,))],
        compiler_params=pltpu.CompilerParams(vmem_limit_bytes=VMEM),
        cost_estimate=pl.CostEstimate(flops=1 << 20, bytes_accessed=4 << 20, transcendentals=0),
    )(*[pltpu.with_memory_space_constraint(v, pltpu.HBM) for v in held])


def scatter_over_columns(x):
    count = lax.axis_size("col")
    pieces = lax.all_to_all(x, "col", 0, 0)
    return jnp.sum(pieces.reshape(count, -1, x.shape[-1]).astype(f32), axis=0).astype(bf16)


def trade_rows(pieces):
    count = lax.axis_size("row") // 2
    groups = [[2 * i + core for i in range(count)] for core in (0, 1)]
    return lax.all_to_all(pieces, "row", 0, 0, axis_index_groups=groups)


def scatter_over_rows(x):
    pieces = trade_rows(x.reshape(lax.axis_size("row") // 2, -1, x.shape[1]))
    return jnp.sum(pieces.astype(f32), axis=0).astype(bf16)


def gather_over_rows(x):
    count = lax.axis_size("row") // 2
    return trade_rows(jnp.broadcast_to(x, (count,) + x.shape)).reshape(-1, x.shape[1])


def per_device(
    tokens,
    gain_fine,
    qkv_fine,
    out_fine,
    w_merge,
    gain_coarse,
    qkv_coarse,
    out_coarse,
    grad_fine,
    grad_coarse,
):
    rows, columns, width = tokens.shape
    crows, ccolumns, cwidth = grad_coarse.shape
    count, ccount = rows * columns, crows * ccolumns
    cols = lax.axis_size("col")
    where = jnp.stack(
        [lax.axis_index("row"), lax.axis_index("col"), lax.axis_size("row"), cols]
    ).astype(jnp.int32)
    factor = 1.0 / math.sqrt(rows * lax.axis_size("row") * columns * cols)
    tok = Late(tokens.reshape(count, width))
    gc = Late(grad_coarse.reshape(ccount, cwidth))
    gain0, gain1 = Late(gain_fine[None, :]), Late(gain_coarse[None, :])
    qkv_fine, out_fine, w_merge = Late(qkv_fine), Late(out_fine), Late(w_merge)
    qkv_coarse, out_coarse = Late(qkv_coarse), Late(out_coarse)

    def moved(piece, dr, dc):
        return [None if p is None else (p[0] + dr, p[1] + dc) for p in piece]

    def chosen(targets, sources):
        return Late(jnp.asarray(one_hot(targets, sources)))

    keys0, keys1 = fine_keys(rows, columns), coarse_keys(crows, ccolumns)
    queries1 = coarse_queries(crows, ccolumns)
    natural = grid_piece(range(rows), range(columns))
    cnatural = queries1[0]
    rim = (2 * RADIUS + 1) * columns
    side, cside = len(keys0[5]), len(queries1[3])
    send_down, send_up = call(
        rows_pack_kernel, [((rim + 2 * ccount, width), bf16)] * 2, flops=1 << 20
    )(tok, gc)
    up = shifted(send_down, "row", 1)
    down = shifted(send_up, "row", -1)
    held = natural + moved(natural[-rim:], -rows, 0) + moved(natural[:rim], rows, 0)
    cheld = cnatural + moved(cnatural, -crows, 0) + moved(cnatural, crows, 0)
    flat0 = joined(keys0)
    own0 = keys0[0]
    asked0 = joined(keys0[:3])
    near = len(keys0[1])
    perm = chosen(own0, natural)
    tok_v, gc_v, picks, cpicks, *ready0 = preload(
        [
            tok,
            gc,
            chosen(moved(keys0[5], 0, columns) + moved(keys0[6], 0, -columns), held),
            chosen(moved(queries1[3], 0, ccolumns) + moved(queries1[4], 0, -ccolumns), cheld),
            perm,
            chosen(merge_order(RADIUS + 1, columns), natural[:near]),
            gain0,
            qkv_fine,
            out_fine,
            w_merge,
            Late(jnp.asarray(band_bias(asked0, flat0))),
            places(flat0),
        ],
        send_up,
    )
    send_right, send_left = call(
        columns_pack_kernel, [((side + 2 * cside, width), bf16)] * 2, flops=1 << 20
    )(
        tok_v,
        gc_v,
        up,
        down,
        picks,
        cpicks,
    )
    left = shifted(send_right, "col", 1)
    right = shifted(send_left, "col", -1)

    merged, near1, down1, up1, field0, query0, kv0, att0 = call(
        fine_forward_kernel,
        [
            ((ccount, 4 * width), bf16),
            ((ccount + near // 2, cwidth), bf16),
            ((ccount, cwidth), bf16),
            ((ccount, cwidth), bf16),
            ((len(flat0), width), bf16),
            ((count, width), bf16),
            ((len(flat0), 2 * width), bf16),
            ((count, width), bf16),
        ],
    )(
        tok_v,
        up,
        down,
        left,
        right,
        *ready0,
        where,
    )

    above1 = shifted(down1, "row", 1)
    below1 = shifted(up1, "row", -1)
    tall1 = joined(keys1[:5])
    wide1 = len(keys1[5])
    flat1, ask1 = joined(keys1), joined(queries1)
    picks1, pick1, gain_v, qkv_v, merge_v, band1, at1, *ready3 = preload(
        [
            chosen(moved(keys1[5], 0, ccolumns) + moved(keys1[6], 0, -ccolumns), tall1),
            chosen(ask1, flat1),
            gain1,
            qkv_coarse,
            w_merge,
            Late(jnp.asarray(band_bias(ask1, flat1))),
            places(flat1),
            Late(grad_fine.reshape(count, width)),
            perm,
            out_fine,
            qkv_fine,
        ],
        near1,
    )
    send_right, send_left = call(
        coarse_pack_kernel, [((wide1, cwidth), bf16)] * 2, flops=1 << 20
    )(
        near1,
        above1,
        below1,
        picks1,
    )
    left1 = shifted(send_right, "col", 1)
    right1 = shifted(send_left, "col", -1)

    flat1, ask1 = joined(keys1), joined(queries1)
    backs = back_keys(rows, columns)
    flatb = joined(backs)
    kvb, normedb, ratiob, *probs = call(
        fine_again_kernel,
        [
            ((len(flatb), 2 * width), bf16),
            ((len(flatb), width), bf16),
            ((len(flatb), width), f32),
        ]
        + [((count, len(flatb)), f32)] * (width // HEAD),
    )(
        query0,
        kv0,
        field0,
        chosen(flatb, flat0),
        gain0,
        Late(jnp.asarray(band_bias(own0, flatb))),
        places(flatb),
        where,
    )
    upstream1, grad_att1 = call(
        coarse_upstream_kernel,
        [((ccount, cwidth), bf16), ((len(ask1), cwidth), bf16)],
    )(
        gc,
        up,
        down,
        left,
        right,
        chosen(ask1, cheld + queries1[3] + queries1[4]),
        out_coarse,
    )
    kept = (4 * width + 2 * cwidth) // 2
    keep1, send1, gain_part1, grad_merged = call(
        coarse_kernel,
        [
            ((ccount, kept), bf16),
            ((ccount, kept + 5 * cwidth), bf16),
            ((1, cwidth), f32),
            ((ccount, 4 * width), f32),
        ],
    )(
        near1,
        above1,
        below1,
        left1,
        right1,
        upstream1,
        grad_att1,
        merged,
        pick1,
        gain_v,
        qkv_v,
        merge_v,
        band1,
        at1,
        where,
    )
    got1 = flip(send1, "row", 1)

    rims = len(backs[1])
    bside = len(backs[3])
    middle = count + 2 * rims
    up0, gq0, mid, left_rim, right_rim, gain_part0, keep0, send0 = call(
        functools.partial(fine_backward_kernel, factor),
        [
            ((count, width), f32),
            ((count, width), bf16),
            ((middle, 2 * width), f32),
            ((bside, 2 * width), bf16),
            ((bside, 2 * width), bf16),
            ((1, width), f32),
            ((width, 2 * width), bf16),
            ((width, 2 * width), bf16),
        ],
    )(
        ready3[0],
        grad_merged,
        ready3[1],
        query0,
        kvb,
        normedb,
        ratiob,
        att0,
        *probs,
        ready3[2],
        ready3[3],
        gain0,
        where,
    )
    n1 = (2 * width + 4 * (cwidth // 2)) // cols
    n0 = width // cols
    (packed,) = call(
        functools.partial(weights_kernel, factor), [((cols, n1 + n0 + 16, cwidth), bf16)]
    )(keep1, send1, got1, keep0, flip(send0, "row", 1), gain_part0, gain_part1)
    sums = scatter_over_columns(packed)
    from_right = shifted(left_rim, "col", -1)
    from_left = shifted(right_rim, "col", 1)
    sums, from_left, from_right = lax.optimization_barrier((sums, from_left, from_right))
    sums = scatter_over_rows(sums)
    mids = joined(backs[:3])
    own, top_rim, bottom_rim = call(
        fine_fold_kernel,
        [((count, 2 * width), f32), ((rims, 2 * width), bf16), ((rims, 2 * width), bf16)],
        flops=1 << 20,
    )(
        mid,
        from_left,
        from_right,
        chosen(mids, moved(backs[4], 0, -columns)),
        chosen(mids, moved(backs[3], 0, columns)),
    )
    x = gather_over_rows(sums)
    x, top_rim, bottom_rim = lax.optimization_barrier((x, top_rim, bottom_rim))
    from_below = shifted(top_rim, "row", -1)
    from_above = shifted(bottom_rim, "row", 1)
    (grad_tokens,) = call(
        fine_last_kernel,
        [
            ((count, width), bf16),
        ],
    )(
        own,
        from_above,
        from_below,
        chosen(own0, moved(backs[2], -rows, 0)),
        chosen(own0, moved(backs[1], rows, 0)),
        gq0,
        up0,
        tok,
        perm,
        gain0,
        qkv_fine,
    )
    x, small = x[:-16], x[-16:]
    x = lax.all_to_all(jnp.broadcast_to(x, (cols,) + x.shape), "col", 0, 0)
    gains = small.astype(f32) + flip(small, "row", 1).astype(f32)
    gain_sums = (gains[1, :width], gains[0])
    x, grad_tokens, gain_sums = lax.optimization_barrier((x, grad_tokens, gain_sums))
    other = flip(x, "row", 1)
    shapes = [
        (2 * cols, 2 * width // cols, cwidth),
        (2 * cols, cwidth // 2 // cols, 3 * cwidth),
        (2 * cols, cwidth // 2 // cols, cwidth),
        (2 * cols, width // 2 // cols, 3 * width),
        (2 * cols, width // 2 // cols, width),
    ]
    vmem = pl.BlockSpec(memory_space=pltpu.VMEM)
    grads = pl.pallas_call(
        unpack_kernel,
        out_shape=[jax.ShapeDtypeStruct(s, bf16) for s in shapes],
        in_specs=[pl.BlockSpec(memory_space=pltpu.SMEM), vmem, vmem],
        out_specs=[pl.BlockSpec(memory_space=pl.ANY)] * len(shapes),
        scratch_shapes=[pltpu.VMEM(s, bf16) for s in shapes]
        + [pltpu.SemaphoreType.DMA((len(shapes),))],
        compiler_params=pltpu.CompilerParams(vmem_limit_bytes=16 << 20),
    )(where, x, other)
    grad_merge, grad_qkv1, grad_out1, grad_qkv0, grad_out0 = (
        g.reshape(-1, g.shape[2]) for g in grads
    )
    return (
        grad_tokens.reshape(rows, columns, width),
        gain_sums[0],
        grad_qkv0,
        grad_out0,
        grad_merge,
        gain_sums[1],
        grad_qkv1,
        grad_out1,
    )


def solution(mesh):
    in_specs = (
        P("row", "col", None),
        P(),
        P(),
        P(),
        P(),
        P(),
        P(),
        P(),
        P("row", "col", None),
        P("row", "col", None),
    )
    out_specs = (P("row", "col", None), P(), P(), P(), P(), P(), P(), P())
    return jax.shard_map(
        per_device, mesh=mesh, in_specs=in_specs, out_specs=out_specs, check_vma=False
    )
```
